32 devices in a mesh: section: 2 (over x), fsdp: 16 (over z, y, core).
Axes of the slice: x: 2, y: 2, z: 4, core: 2. Of those that a mesh axis runs over, the one named last changes fastest.
Arguments:
- inputs: bfloat16 [2, 2, 2048, 2048], P(None, 'section', 'fsdp'), may hold values from -6 to 6
- top_grad: bfloat16 [2, 2048, 2048], P('section', 'fsdp'), may hold values from -6 to 6
- gains: float32 [2, 2048], P('section', 'fsdp'), may hold values from 0.25 to 1.75
- short_filters: float32 [2, 3, 7, 2048], P('section', None, None, 'fsdp'), may hold values from -2 to 2
- medium_filters: float32 [2, 128, 128], P('section', None, 'fsdp'), may hold values from -0.5 to 0.5
- lower_gain: float32 [2048], P('fsdp'), may hold values from 0.25 to 1.75
- lower_short: float32 [3, 7, 2048], P(None, None, 'fsdp'), may hold values from -2 to 2
- lower_medium: float32 [128, 128], P(None, 'fsdp'), may hold values from -0.5 to 0.5
Outputs:
- window_grads: bfloat16 [2, 2048, 2048], P('section', 'fsdp')
- gain_grads: float32 [2, 2048], P('section', 'fsdp')
- short_grads: float32 [2, 3, 7, 2048], P('section', None, None, 'fsdp')
- medium_grads: float32 [2, 128, 128], P('section', None, 'fsdp')
The draws below stay inside these ranges and needn't reach their ends.
All inputs are finite; a program needn't handle non-finite values.
Results may differ from the reference program's by a relative error of at most 0.011.
Values may be sent and summed in bfloat16 or wider, within the bound.
A program may use at most 192 MiB of HBM per device.

```python
import jax
import jax.numpy as jnp
from jax import lax

D = 2048
TAPS = 128
SHORT = 7
CH_GROUP = 16
GROUPS = 128
TOKENS = 2048
MICRO = 2


def with_spikes(drawn, key, source, target, parts, factor):
    owner, partner = [(jnp.arange(drawn.shape[dim]) // (drawn.shape[dim] // parts)).reshape([-1 if axis == dim else 1 for axis in range(drawn.ndim)]) for dim in (source, target)]
    chosen = jax.random.permutation(key, parts)[partner]
    strong = (owner == chosen) | (owner == (partner + parts // 2) % parts)
    return jnp.where(strong, factor * drawn, drawn)


def steps_of(rng, extent, shards, least, top_value):
    loudness, own = 1.0, jax.random.fold_in(rng, 6)
    for position, blocks in shards:
        steps = jnp.exp(jax.random.uniform(jax.random.fold_in(own, position), (blocks,), jnp.float32, least / len(shards), top_value / len(shards)))
        loudness = loudness * jnp.repeat(steps, extent[position] // blocks).reshape([-1 if axis == position else 1 for axis in range(len(extent))])
    return loudness


def scatter_about(rng, extent, width, most, shards=(), held_as=jnp.bfloat16):
    factor_of = steps_of(rng, extent, shards, -0.22, 0.18) if shards else 1.0
    result = jax.random.normal(rng, extent, jnp.float32) * width * factor_of
    return jnp.minimum(jnp.maximum(result, -most), most).astype(held_as)


def gaussian_with(key, dims, deviation, most, shards, heavy, kind=jnp.bfloat16):
    values = deviation * jax.random.normal(key, dims, jnp.float32)
    if shards:
        values = values * steps_of(key, dims, shards, -0.22, 0.18)
    return jnp.clip(with_spikes(values, jax.random.fold_in(key, 3), *heavy), -most, most).astype(kind)


def setup_inputs(seed: int = 0) -> dict:
    arg_keys = jax.random.split(jax.random.key(seed), 9)
    inputs = gaussian_with(arg_keys[0], (2, MICRO, TOKENS, D), 1.0, 6.0, ((1, 2), (2, 16)), (2, 3, 16, 2.0))
    top_grad = scatter_about(arg_keys[1], (MICRO, TOKENS, D), 1.0, 6.0, ((0, 2), (1, 16)))
    gains = jnp.clip(1.0 + 0.15 * jax.random.normal(arg_keys[2], (MICRO, D), jnp.float32), 0.25, 1.75)
    short_filters = scatter_about(arg_keys[3], (MICRO, 3, SHORT, D), SHORT ** -0.5, 2.0, ((0, 2), (3, 16)), jnp.float32)
    medium_filters = scatter_about(arg_keys[4], (MICRO, GROUPS, TAPS), TAPS ** -0.5, 0.5, ((0, 2), (2, 16)), jnp.float32)
    lower_gain = jnp.clip(1.0 + 0.15 * jax.random.normal(arg_keys[5], (D,), jnp.float32), 0.25, 1.75)
    lower_short = scatter_about(arg_keys[6], (3, SHORT, D), SHORT ** -0.5, 2.0, ((2, 16),), jnp.float32)
    lower_medium = scatter_about(arg_keys[7], (GROUPS, TAPS), TAPS ** -0.5, 0.5, ((1, 16),), jnp.float32)
    return dict(inputs=inputs, top_grad=top_grad, gains=gains, short_filters=short_filters, medium_filters=medium_filters, lower_gain=lower_gain, lower_short=lower_short, lower_medium=lower_medium)


NORM_EPS = 1e-06
HIGHEST_MODE = lax.Precision.HIGHEST

def rounded(source_array):
    return lax.optimization_barrier(source_array.astype(jnp.bfloat16))

def move_rows(source_array, amount):
    row_count = source_array.shape[0]
    if amount == 0:
        return source_array
    filler = jnp.zeros((abs(amount),) + source_array.shape[1:], source_array.dtype)
    if amount > 0:
        return jnp.concatenate([filler, source_array[:row_count - amount]], 0)
    return jnp.concatenate([source_array[-amount:], filler], 0)

def lag_tables(taps_f):
    tap_count = taps_f.shape[1]
    row_ids = jnp.arange(tap_count)[:, None]
    col_ids = jnp.arange(tap_count)[None, :]
    near_lag = row_ids - col_ids
    far_lag = near_lag + tap_count
    near_vals = taps_f[:, jnp.clip(near_lag, 0, tap_count - 1)]
    far_vals = taps_f[:, jnp.clip(far_lag, 0, tap_count - 1)]
    near_table = jnp.where(near_lag >= 0, near_vals, jnp.zeros_like(near_vals))
    far_table = jnp.where(far_lag <= tap_count - 1, far_vals, jnp.zeros_like(far_vals))
    return (near_table, far_table)

def in_blocks(source_array, tap_count):
    row_count, col_count = source_array.shape
    return source_array.reshape(row_count // tap_count, tap_count, col_count // CH_GROUP, CH_GROUP)

def causal_mix(signal, near_table, far_table):
    blocks = in_blocks(signal, near_table.shape[1])
    before = jnp.concatenate([jnp.zeros_like(blocks[:1]), blocks[:-1]], 0)
    mixed_rows = jnp.einsum('gts,bsgc->btgc', near_table, blocks, precision=HIGHEST_MODE)
    mixed_rows = mixed_rows + jnp.einsum('gts,bsgc->btgc', far_table, before, precision=HIGHEST_MODE)
    return mixed_rows.reshape(signal.shape)

def anticausal_mix(signal, near_table, far_table):
    blocks = in_blocks(signal, near_table.shape[1])
    next_blocks = jnp.concatenate([blocks[1:], jnp.zeros_like(blocks[:1])], 0)
    mixed_rows = jnp.einsum('gts,btgc->bsgc', near_table, blocks, precision=HIGHEST_MODE)
    mixed_rows = mixed_rows + jnp.einsum('gts,btgc->bsgc', far_table, next_blocks, precision=HIGHEST_MODE)
    return mixed_rows.reshape(signal.shape)

def lag_sums(grad_f, signal, tap_count):
    grad_blocks = in_blocks(grad_f, tap_count)
    sig_blocks = in_blocks(signal, tap_count)
    before = jnp.concatenate([jnp.zeros_like(sig_blocks[:1]), sig_blocks[:-1]], 0)
    same_block = jnp.einsum('btgc,bsgc->gts', grad_blocks, sig_blocks, precision=HIGHEST_MODE)
    cross_block = jnp.einsum('btgc,bsgc->gts', grad_blocks, before, precision=HIGHEST_MODE)
    row_ids = jnp.arange(tap_count)[:, None, None]
    col_ids = jnp.arange(tap_count)[None, :, None]
    tap_ids = jnp.arange(tap_count)[None, None, :]
    near_pick = jnp.where(row_ids - col_ids == tap_ids, 1.0, 0.0).astype(same_block.dtype)
    far_pick = jnp.where(row_ids - col_ids + tap_count == tap_ids, 1.0, 0.0).astype(same_block.dtype)
    return jnp.einsum('gts,tsi->gi', same_block, near_pick, precision=HIGHEST_MODE) + jnp.einsum('gts,tsi->gi', cross_block, far_pick, precision=HIGHEST_MODE)

def layer_grads(layer_in, cotangent, gain, short_taps, medium_taps):
    in_f = layer_in.astype(jnp.float32)
    scale_rows = lax.rsqrt(lax.optimization_barrier(jnp.mean(in_f * in_f, axis=-1, keepdims=True)) + NORM_EPS)
    normed = in_f * scale_rows * gain
    branches = []
    for branch in range(3):
        running = short_taps[branch, 0] * normed
        for offset in range(1, SHORT):
            running = running + short_taps[branch, offset] * move_rows(normed, offset)
        branches.append(running)
    query_rows, key_rows, value_rows = branches
    product_f = rounded(key_rows * value_rows).astype(jnp.float32)
    taps_b = rounded(medium_taps).astype(jnp.float32)
    near_table, far_table = lag_tables(taps_b)
    filtered = causal_mix(product_f, near_table, far_table)
    cot_f = cotangent.astype(jnp.float32)
    grad_filtered = rounded(cot_f * query_rows).astype(jnp.float32)
    grad_product = anticausal_mix(grad_filtered, near_table, far_table)
    stacked = rounded(jnp.stack([cot_f * filtered, grad_product * value_rows, grad_product * key_rows])).astype(jnp.float32)
    grad_normed = jnp.zeros_like(normed)
    for branch in range(3):
        for offset in range(SHORT):
            grad_normed = grad_normed + short_taps[branch, offset] * move_rows(stacked[branch], -offset)
    scaled = gain * grad_normed
    inner_mean = lax.optimization_barrier(jnp.mean(in_f * scaled, axis=-1, keepdims=True))
    grad_in = rounded(cot_f + scale_rows * scaled - in_f * scale_rows ** 3 * inner_mean)
    grad_gain = lax.optimization_barrier(jnp.sum(grad_normed * in_f * scale_rows, axis=0))
    grad_short = jnp.stack([jnp.stack([lax.optimization_barrier(jnp.sum(stacked[branch] * move_rows(normed, offset), axis=0)) for offset in range(SHORT)]) for branch in range(3)])
    grad_medium = lag_sums(grad_filtered, product_f, medium_taps.shape[1])
    return (grad_in, grad_gain, grad_short, grad_medium)

def reference(inputs, top_grad, gains, short_filters, medium_filters, lower_gain, lower_short, lower_medium):
    section_count = inputs.shape[1]
    first_grads = []
    gain_terms = []
    short_terms = []
    medium_terms = []
    for section_id in range(section_count):
        grad_in, grad_gain, grad_short, grad_medium = layer_grads(inputs[0, section_id], top_grad[section_id], gains[section_id], short_filters[section_id], medium_filters[section_id])
        first_grads.append(grad_in)
        gain_terms.append(grad_gain)
        short_terms.append(grad_short)
        medium_terms.append(grad_medium)
    window = []
    for section_id in range(section_count):
        source = (section_id + 1) % section_count
        if section_id == section_count - 1:
            grad_in, grad_gain, grad_short, grad_medium = layer_grads(inputs[1, section_id], first_grads[source], lower_gain, lower_short, lower_medium)
        else:
            grad_in, grad_gain, grad_short, grad_medium = layer_grads(inputs[1, section_id], first_grads[source], gains[section_id], short_filters[section_id], medium_filters[section_id])
            gain_terms[section_id] = gain_terms[section_id] + grad_gain
            short_terms[section_id] = short_terms[section_id] + grad_short
            medium_terms[section_id] = medium_terms[section_id] + grad_medium
        window.append(grad_in)
    factor = TOKENS ** (-0.5)
    return (jnp.stack(window), jnp.stack(gain_terms) * factor, jnp.stack(short_terms) * factor, jnp.stack(medium_terms) * factor)
```

```python
import jax
import jax.numpy as jnp
from jax import lax
from jax.experimental import pallas as pl
from jax.experimental.pallas import tpu as pltpu
from jax.sharding import PartitionSpec as P

TAPS = 128
SHORT = 7
CH_GROUP = 16
NORM_EPS = 1e-06
LANES = 128
PER = LANES // CH_GROUP
EDGE = 16
F32 = jnp.float32
BF16 = jnp.bfloat16
PARAMS = dict(vmem_limit_bytes=48 * 2**20)


def toeplitz(row, rows):
    wide = jnp.broadcast_to(row, (rows, 2 * TAPS))
    return pltpu.roll(wide, 0, 1, stride=1, stride_axis=0).astype(BF16)


def band(table_ref, signal_ref):
    head = signal_ref[: 2 * TAPS]
    tail = signal_ref[TAPS : 3 * TAPS]
    group = lax.broadcasted_iota(jnp.int32, (TAPS, LANES), 1) // CH_GROUP
    group_edge = lax.broadcasted_iota(jnp.int32, (EDGE, LANES), 1) // CH_GROUP
    main = jnp.zeros((TAPS, LANES), F32)
    edge = jnp.zeros((EDGE, LANES), F32)
    edges = []
    for g in range(PER):
        table = toeplitz(table_ref[g : g + 1, :], TAPS)
        edges.append(table[:EDGE])
        part = jnp.dot(table, head, preferred_element_type=F32)
        main = jnp.where(group == g, part, main)
    parts = jnp.dot(jnp.concatenate(edges, 0), tail, preferred_element_type=F32)
    for g in range(PER):
        edge = jnp.where(group_edge == g, parts[g * EDGE : (g + 1) * EDGE], edge)
    return main, edge


def forward_kernel(
    x_ref, r_ref, gain_ref, short_ref, table_ref, q_ref, k_ref, v_ref, u_ref, w_ref, g_ref, us, ws
):
    total = x_ref.shape[0]
    own = TAPS + EDGE
    us[...] = x_ref[...].astype(F32) * r_ref[...] * gain_ref[...]
    u_ref[...] = us[TAPS : TAPS + own]
    half = (2 * TAPS + EDGE) // 2
    for part in range(2):
        low = part * half
        acc = None
        for j in range(SHORT):
            add = short_ref[j : j + 1, :] * us[own + low - j : own + low - j + half]
            acc = add if acc is None else acc + add
        q_ref[low : low + half] = acc
    for low, size in ((0, TAPS), (TAPS, own)):
        keys, values = None, None
        for j in range(SHORT):
            rows = us[EDGE + low - j : EDGE + low - j + size]
            key = short_ref[SHORT + j : SHORT + j + 1, :] * rows
            value = short_ref[2 * SHORT + j : 2 * SHORT + j + 1, :] * rows
            keys = key if keys is None else keys + key
            values = value if values is None else values + value
        ws[low : low + size] = (keys * values).astype(BF16)
        if low:
            k_ref[...] = keys
            v_ref[...] = values
    ws[2 * TAPS + EDGE :] = jnp.zeros((TAPS - EDGE, LANES), BF16)
    w_ref[...] = ws[: 2 * TAPS]
    main, edge = band(table_ref, ws)
    g_ref[:TAPS] = main
    g_ref[TAPS:] = edge


def backward_kernel(
    e_ref, q_ref, k_ref, v_ref, g_ref, xf_ref, x_ref, r_ref, gain_ref, short_ref, table_ref,
    dx_ref, dg_ref, da_ref, du_ref, dgs, das, held, means,
):
    step = pl.program_id(0)
    steps = pl.num_programs(0)
    own = TAPS + EDGE
    dgs[: TAPS + own] = (e_ref[...].astype(F32) * q_ref[...]).astype(BF16)
    dgs[TAPS + own :] = jnp.zeros((TAPS - EDGE, LANES), BF16)
    dg_ref[...] = dgs[:TAPS]
    main, edge = band(table_ref, dgs)
    for low, size, dw in ((0, TAPS, main), (TAPS, EDGE, edge)):
        rows = slice(low, low + size)
        das[0, rows] = (e_ref[rows].astype(F32) * g_ref[rows]).astype(BF16).astype(F32)
        das[1, rows] = (dw * v_ref[rows]).astype(BF16).astype(F32)
        das[2, rows] = (dw * k_ref[rows]).astype(BF16).astype(F32)
    da_ref[...] = das[:, :TAPS].astype(BF16)
    acc = None
    for c in range(3):
        for j in range(SHORT):
            add = short_ref[SHORT * c + j : SHORT * c + j + 1, :] * das[c, j : j + TAPS]
            acc = add if acc is None else acc + add
    du_ref[...] = acc
    scaled = gain_ref[...] * acc
    part = jnp.sum(x_ref[...].astype(F32) * scaled, axis=1, keepdims=True)

    @pl.when(step == 0)
    def _():
        means[...] = jnp.zeros_like(means)

    means[...] += part
    held[step] = e_ref[:TAPS].astype(F32) + r_ref[...] * scaled

    @pl.when(step == steps - 1)
    def _():
        r = r_ref[...]
        factor = r * r * r * (means[...] * (1.0 / dx_ref.shape[1]))
        for b in range(dx_ref.shape[1] // LANES):
            lanes = slice(b * LANES, (b + 1) * LANES)
            dx_ref[:, lanes] = (held[b] - xf_ref[:, lanes].astype(F32) * factor).astype(BF16)


def terms_kernel(
    dg_ref, da_ref, du_ref, u_ref, w_ref, x_ref, r_ref, tg_ref, ts_ref, tm_ref
):
    tg_ref[...] = jnp.sum(du_ref[...] * x_ref[...].astype(F32) * r_ref[...], axis=0, keepdims=True)
    for c in range(3):
        grads = da_ref[c].astype(F32)
        for j in range(SHORT):
            row = SHORT * c + j
            ts_ref[row : row + 1, :] = jnp.sum(
                grads * u_ref[EDGE - j : EDGE - j + TAPS], axis=0, keepdims=True
            )
    ts_ref[3 * SHORT :, :] = jnp.zeros((3, LANES), F32)
    grads = dg_ref[...].astype(F32)
    mask = (
        lax.broadcasted_iota(jnp.int32, (1, PER, LANES), 2) // CH_GROUP
        == lax.broadcasted_iota(jnp.int32, (1, PER, LANES), 1)
    )
    spread = jnp.where(mask, jnp.broadcast_to(grads[:, None, :], (TAPS, PER, LANES)), 0.0)
    spread = spread.reshape(TAPS * PER, LANES).astype(BF16)
    lags = lax.dot_general(
        spread, w_ref[...], (((1,), (1,)), ((), ())), preferred_element_type=F32
    )
    total = lags[:PER]
    for t in range(1, TAPS):
        total = total + pltpu.roll(lags[t * PER : (t + 1) * PER], 2 * TAPS - t, 1)
    tm_ref[...] = total


def tall(rows, dtype=F32):
    return pl.BlockSpec((rows, LANES), lambda i: (0, i))


def whole(shape):
    return pl.BlockSpec(shape, lambda i: (0,) * len(shape))


GROUP_SPEC = pl.BlockSpec((PER, 2 * TAPS), lambda i: (i, 0))
BRANCH_SPEC = pl.BlockSpec((3, TAPS, LANES), lambda i: (0, 0, i))


def run_forward(x_ext, r_ext, gain, short, table):
    total, channels = x_ext.shape
    own = TAPS + EDGE
    shapes = [
        ((TAPS + own), F32), (own, F32), (own, F32), (own, F32), (2 * TAPS, BF16), (own, F32),
    ]
    return pl.pallas_call(
        forward_kernel,
        grid=(channels // LANES,),
        in_specs=[tall(total), whole((total, 1)), tall(1), tall(24), GROUP_SPEC],
        out_specs=[tall(rows) for rows, _ in shapes],
        out_shape=[jax.ShapeDtypeStruct((rows, channels), kind) for rows, kind in shapes],
        scratch_shapes=[pltpu.VMEM((total, LANES), F32), pltpu.VMEM((3 * TAPS, LANES), BF16)],
        compiler_params=pltpu.CompilerParams(**PARAMS),
        cost_estimate=pl.CostEstimate(flops=4 * 10**9, bytes_accessed=12 * 10**6, transcendentals=0),
    )(x_ext, r_ext, gain, short, table)


def run_backward(e_ext, q, k, v, g, x, r, gain, short, table):
    channels = x.shape[1]
    own = TAPS + EDGE
    blocks = channels // LANES
    return pl.pallas_call(
        backward_kernel,
        grid=(blocks,),
        in_specs=[
            tall(TAPS + own), tall(TAPS + own), tall(own), tall(own), tall(own),
            whole((TAPS, channels)), tall(TAPS), whole((TAPS, 1)), tall(1), tall(24), GROUP_SPEC,
        ],
        out_specs=[whole((TAPS, channels)), tall(TAPS), BRANCH_SPEC, tall(TAPS)],
        out_shape=[
            jax.ShapeDtypeStruct((TAPS, channels), BF16),
            jax.ShapeDtypeStruct((TAPS, channels), BF16),
            jax.ShapeDtypeStruct((3, TAPS, channels), BF16),
            jax.ShapeDtypeStruct((TAPS, channels), F32),
        ],
        scratch_shapes=[
            pltpu.VMEM((3 * TAPS, LANES), BF16),
            pltpu.VMEM((3, own, LANES), F32),
            pltpu.VMEM((blocks, TAPS, LANES), F32),
            pltpu.VMEM((TAPS, 1), F32),
        ],
        compiler_params=pltpu.CompilerParams(**PARAMS),
        cost_estimate=pl.CostEstimate(flops=4 * 10**9, bytes_accessed=12 * 10**6, transcendentals=0),
    )(e_ext, q, k, v, g, x, x, r, gain, short, table)


def run_terms(dg, da, du, u, w, x, r):
    channels = x.shape[1]
    return pl.pallas_call(
        terms_kernel,
        grid=(channels // LANES,),
        in_specs=[
            tall(TAPS), BRANCH_SPEC, tall(TAPS), tall(TAPS + EDGE), tall(2 * TAPS), tall(TAPS),
            whole((TAPS, 1)),
        ],
        out_specs=[tall(1), tall(24), GROUP_SPEC],
        out_shape=[
            jax.ShapeDtypeStruct((1, channels), F32),
            jax.ShapeDtypeStruct((24, channels), F32),
            jax.ShapeDtypeStruct((channels // CH_GROUP, 2 * TAPS), F32),
        ],
        compiler_params=pltpu.CompilerParams(**PARAMS),
        cost_estimate=pl.CostEstimate(flops=4 * 10**9, bytes_accessed=8 * 10**6, transcendentals=0),
    )(dg, da, du, u, w, x, r)


def shifted(value, steps):
    count = lax.axis_size("fsdp")
    initial, last = (max(0, -steps), min(count, count - steps))
    return lax.ppermute(value, "fsdp", [(source, source + steps) for source in range(initial, last)])


def crossed(value, steps):
    sections, count = lax.axis_size("section"), lax.axis_size("fsdp")
    pairs = [
        (s * count + f, ((s - 1) % sections) * count + f - steps)
        for s in range(sections)
        for f in range(steps, count)
    ]
    return lax.ppermute(value, ("section", "fsdp"), pairs)


def on_device(
    inputs, top_grad, gains, short_filters, medium_filters, lower_gain, lower_short, lower_medium
):
    shards = lax.axis_size("fsdp")
    last_section = lax.axis_index("section") == lax.axis_size("section") - 1
    chunk = gains.shape[1]
    channels = chunk * shards
    flat = jnp.stack(
        [
            jnp.concatenate([gains.reshape(-1), short_filters.reshape(-1), medium_filters.reshape(-1)]),
            jnp.concatenate([lower_gain, lower_short.reshape(-1), lower_medium.reshape(-1)]),
        ]
    )
    every = lax.all_gather(flat, "fsdp", axis=0, tiled=False)

    def layer_params(part):
        gain = part[:, :chunk].reshape(1, channels)
        short = jnp.transpose(
            part[:, chunk : 22 * chunk].reshape(shards, 3 * SHORT, chunk), (1, 0, 2)
        ).reshape(3 * SHORT, channels)
        medium = jnp.transpose(
            part[:, 22 * chunk :].reshape(shards, -1, TAPS // shards), (1, 0, 2)
        ).reshape(-1, TAPS)
        medium = medium.astype(BF16).astype(F32)
        short = jnp.pad(short, ((0, 3), (0, 0)))
        causal = jnp.pad(medium[:, ::-1], ((0, 0), (1, TAPS - 1)))
        anti = jnp.pad(medium, ((0, 0), (0, TAPS)))
        return gain, short, causal, anti

    upper = every[:, 0]
    params = (layer_params(upper), layer_params(jnp.where(last_section, every[:, 1], upper)))

    def extended(x):
        rows = x.shape[0]
        x_ext = jnp.concatenate(
            [
                shifted(x[rows - EDGE :], 2), shifted(x, 1), x, shifted(x, -1),
                shifted(x[:EDGE], -2),
            ]
        )
        wide = x_ext.astype(F32)
        r_ext = lax.rsqrt(jnp.mean(wide * wide, axis=-1, keepdims=True) + NORM_EPS)
        return x_ext, r_ext

    def terms_of(x, r, ahead, back):
        return run_terms(back[1], back[2], back[3], ahead[3], ahead[4], x, r)

    x1, x2, e1 = inputs[0, 0], inputs[1, 0], top_grad[0]
    e1_ext = jnp.concatenate([e1, shifted(e1, -1), shifted(e1[:EDGE], -2)])
    x1_ext, r1_ext = extended(x1)
    x2_ext, r2_ext = extended(x2)
    own_rows = slice(TAPS + EDGE, 2 * TAPS + EDGE)
    r1, r2 = r1_ext[own_rows], r2_ext[own_rows]
    (gain1, short1, causal1, anti1), (gain2, short2, causal2, anti2) = params
    ahead1 = run_forward(x1_ext, r1_ext, gain1, short1, causal1)
    back1 = run_backward(
        e1_ext, ahead1[0], ahead1[1], ahead1[2], ahead1[5], x1, r1, gain1, short1, anti1
    )
    dx1 = back1[0]
    e2_ext = jnp.concatenate([crossed(dx1, 0), crossed(dx1, 1), crossed(dx1[:EDGE], 2)])
    ahead2 = run_forward(x2_ext, r2_ext, gain2, short2, causal2)
    terms1 = terms_of(x1, r1, ahead1, back1)
    back2 = run_backward(
        e2_ext, ahead2[0], ahead2[1], ahead2[2], ahead2[5], x2, r2, gain2, short2, anti2
    )
    terms2 = terms_of(x2, r2, ahead2, back2)
    keep = jnp.where(last_section, 0.0, 1.0)
    tg, ts, tm = [a + keep * b for a, b in zip(terms1, terms2)]
    ts = jnp.transpose(ts[: 3 * SHORT].reshape(3 * SHORT, shards, chunk), (1, 0, 2))
    tm = tm[:, 1 : TAPS + 1][:, ::-1]
    groups = tm.shape[0]
    tm = jnp.transpose(tm.reshape(groups, shards, TAPS // shards), (1, 0, 2))
    packed = jnp.concatenate(
        [tg.reshape(shards, chunk), ts.reshape(shards, -1), tm.reshape(shards, -1)], axis=1
    )
    factor = (x1.shape[0] * shards) ** (-0.5)
    width = packed.shape[1]
    room = -(-width // 1024) * 1024
    packed = jnp.pad(packed, ((0, 0), (0, room - width))).reshape(shards * room)
    summed = lax.psum_scatter(packed, "fsdp", scatter_dimension=0, tiled=True) * factor
    return (
        back2[0][None],
        summed[:chunk][None],
        summed[chunk : 22 * chunk].reshape(1, 3, SHORT, chunk),
        summed[22 * chunk : 30 * chunk].reshape(1, groups, TAPS // shards),
    )


def solution(mesh):
    in_specs = (
        P(None, "section", "fsdp", None),
        P("section", "fsdp", None),
        P("section", "fsdp"),
        P("section", None, None, "fsdp"),
        P("section", None, "fsdp"),
        P("fsdp"),
        P(None, None, "fsdp"),
        P(None, "fsdp"),
    )
    out_specs = (
        P("section", "fsdp", None),
        P("section", "fsdp"),
        P("section", None, None, "fsdp"),
        P("section", None, "fsdp"),
    )
    return jax.shard_map(
        on_device, mesh=mesh, in_specs=in_specs, out_specs=out_specs, check_vma=False
    )
```

```python
import jax
import jax.numpy as jnp
from jax import lax
from jax.experimental import pallas as pl
from jax.experimental.pallas import tpu as pltpu
from jax.sharding import PartitionSpec as P

TAPS = 128
SHORT = 7
CH_GROUP = 16
NORM_EPS = 1e-06
LANES = 128
PER = LANES // CH_GROUP
EDGE = 16
F32 = jnp.float32
BF16 = jnp.bfloat16
PARAMS = dict(vmem_limit_bytes=48 * 2**20)


def toeplitz(row, rows):
    wide = jnp.broadcast_to(row, (rows, 2 * TAPS))
    return pltpu.roll(wide, 0, 1, stride=1, stride_axis=0).astype(BF16)


def band(table_ref, signal_ref):
    head = signal_ref[: 2 * TAPS]
    tail = signal_ref[TAPS : 3 * TAPS]
    group = lax.broadcasted_iota(jnp.int32, (TAPS, LANES), 1) // CH_GROUP
    group_edge = lax.broadcasted_iota(jnp.int32, (EDGE, LANES), 1) // CH_GROUP
    main = jnp.zeros((TAPS, LANES), F32)
    edge = jnp.zeros((EDGE, LANES), F32)
    edges = []
    for g in range(PER):
        table = toeplitz(table_ref[g : g + 1, :], TAPS)
        edges.append(table[:EDGE])
        part = jnp.dot(table, head, preferred_element_type=F32)
        main = jnp.where(group == g, part, main)
    parts = jnp.dot(jnp.concatenate(edges, 0), tail, preferred_element_type=F32)
    for g in range(PER):
        edge = jnp.where(group_edge == g, parts[g * EDGE : (g + 1) * EDGE], edge)
    return main, edge


def forward_kernel(
    x_ref, r_ref, gain_ref, short_ref, table_ref, q_ref, k_ref, v_ref, u_ref, w_ref, g_ref, us, ws
):
    total = x_ref.shape[0]
    own = TAPS + EDGE
    us[...] = x_ref[...].astype(F32) * r_ref[...] * gain_ref[...]
    u_ref[...] = us[TAPS : TAPS + own]
    half = (2 * TAPS + EDGE) // 2
    for part in range(2):
        low = part * half
        acc = None
        for j in range(SHORT):
            add = short_ref[j : j + 1, :] * us[own + low - j : own + low - j + half]
            acc = add if acc is None else acc + add
        q_ref[low : low + half] = acc
    for low, size in ((0, TAPS), (TAPS, own)):
        keys, values = None, None
        for j in range(SHORT):
            rows = us[EDGE + low - j : EDGE + low - j + size]
            key = short_ref[SHORT + j : SHORT + j + 1, :] * rows
            value = short_ref[2 * SHORT + j : 2 * SHORT + j + 1, :] * rows
            keys = key if keys is None else keys + key
            values = value if values is None else values + value
        ws[low : low + size] = (keys * values).astype(BF16)
        if low:
            k_ref[...] = keys
            v_ref[...] = values
    ws[2 * TAPS + EDGE :] = jnp.zeros((TAPS - EDGE, LANES), BF16)
    w_ref[...] = ws[: 2 * TAPS]
    main, edge = band(table_ref, ws)
    g_ref[:TAPS] = main
    g_ref[TAPS:] = edge


def backward_kernel(
    e_ref, q_ref, k_ref, v_ref, g_ref, xf_ref, x_ref, r_ref, gain_ref, short_ref, table_ref,
    dx_ref, dg_ref, da_ref, du_ref, dgs, das, held, means,
):
    step = pl.program_id(0)
    steps = pl.num_programs(0)
    own = TAPS + EDGE
    dgs[: TAPS + own] = (e_ref[...].astype(F32) * q_ref[...]).astype(BF16)
    dgs[TAPS + own :] = jnp.zeros((TAPS - EDGE, LANES), BF16)
    dg_ref[...] = dgs[:TAPS]
    main, edge = band(table_ref, dgs)
    for low, size, dw in ((0, TAPS, main), (TAPS, EDGE, edge)):
        rows = slice(low, low + size)
        das[0, rows] = (e_ref[rows].astype(F32) * g_ref[rows]).astype(BF16).astype(F32)
        das[1, rows] = (dw * v_ref[rows]).astype(BF16).astype(F32)
        das[2, rows] = (dw * k_ref[rows]).astype(BF16).astype(F32)
    da_ref[...] = das[:, :TAPS].astype(BF16)
    acc = None
    for c in range(3):
        for j in range(SHORT):
            add = short_ref[SHORT * c + j : SHORT * c + j + 1, :] * das[c, j : j + TAPS]
            acc = add if acc is None else acc + add
    du_ref[...] = acc
    scaled = gain_ref[...] * acc
    part = jnp.sum(x_ref[...].astype(F32) * scaled, axis=1, keepdims=True)

    @pl.when(step == 0)
    def _():
        means[...] = jnp.zeros_like(means)

    means[...] += part
    held[step] = e_ref[:TAPS].astype(F32) + r_ref[...] * scaled

    @pl.when(step == steps - 1)
    def _():
        r = r_ref[...]
        factor = r * r * r * (means[...] * (1.0 / dx_ref.shape[1]))
        for b in range(dx_ref.shape[1] // LANES):
            lanes = slice(b * LANES, (b + 1) * LANES)
            dx_ref[:, lanes] = (held[b] - xf_ref[:, lanes].astype(F32) * factor).astype(BF16)


def terms_kernel(
    dg_ref, da_ref, du_ref, u_ref, w_ref, x_ref, r_ref, tg_ref, ts_ref, tm_ref
):
    tg_ref[...] = jnp.sum(du_ref[...] * x_ref[...].astype(F32) * r_ref[...], axis=0, keepdims=True)
    for c in range(3):
        grads = da_ref[c].astype(F32)
        for j in range(SHORT):
            row = SHORT * c + j
            ts_ref[row : row + 1, :] = jnp.sum(
                grads * u_ref[EDGE - j : EDGE - j + TAPS], axis=0, keepdims=True
            )
    ts_ref[3 * SHORT :, :] = jnp.zeros((3, LANES), F32)
    grads = dg_ref[...].astype(F32)
    mask = (
        lax.broadcasted_iota(jnp.int32, (1, PER, LANES), 2) // CH_GROUP
        == lax.broadcasted_iota(jnp.int32, (1, PER, LANES), 1)
    )
    spread = jnp.where(mask, jnp.broadcast_to(grads[:, None, :], (TAPS, PER, LANES)), 0.0)
    spread = spread.reshape(TAPS * PER, LANES).astype(BF16)
    lags = lax.dot_general(
        spread, w_ref[...], (((1,), (1,)), ((), ())), preferred_element_type=F32
    )
    total = lags[:PER]
    for t in range(1, TAPS):
        total = total + pltpu.roll(lags[t * PER : (t + 1) * PER], 2 * TAPS - t, 1)
    tm_ref[...] = total


def tall(rows, dtype=F32):
    return pl.BlockSpec((rows, LANES), lambda i: (0, i))


def whole(shape):
    return pl.BlockSpec(shape, lambda i: (0,) * len(shape))


GROUP_SPEC = pl.BlockSpec((PER, 2 * TAPS), lambda i: (i, 0))
BRANCH_SPEC = pl.BlockSpec((3, TAPS, LANES), lambda i: (0, 0, i))


def run_forward(x_ext, r_ext, gain, short, table):
    total, channels = x_ext.shape
    own = TAPS + EDGE
    shapes = [
        ((TAPS + own), F32), (own, F32), (own, F32), (own, F32), (2 * TAPS, BF16), (own, F32),
    ]
    return pl.pallas_call(
        forward_kernel,
        grid=(channels // LANES,),
        in_specs=[tall(total), whole((total, 1)), tall(1), tall(24), GROUP_SPEC],
        out_specs=[tall(rows) for rows, _ in shapes],
        out_shape=[jax.ShapeDtypeStruct((rows, channels), kind) for rows, kind in shapes],
        scratch_shapes=[pltpu.VMEM((total, LANES), F32), pltpu.VMEM((3 * TAPS, LANES), BF16)],
        compiler_params=pltpu.CompilerParams(**PARAMS),
        cost_estimate=pl.CostEstimate(flops=4 * 10**9, bytes_accessed=12 * 10**6, transcendentals=0),
    )(x_ext, r_ext, gain, short, table)


def run_backward(e_ext, q, k, v, g, x, r, gain, short, table):
    channels = x.shape[1]
    own = TAPS + EDGE
    blocks = channels // LANES
    return pl.pallas_call(
        backward_kernel,
        grid=(blocks,),
        in_specs=[
            tall(TAPS + own), tall(TAPS + own), tall(own), tall(own), tall(own),
            whole((TAPS, channels)), tall(TAPS), whole((TAPS, 1)), tall(1), tall(24), GROUP_SPEC,
        ],
        out_specs=[whole((TAPS, channels)), tall(TAPS), BRANCH_SPEC, tall(TAPS)],
        out_shape=[
            jax.ShapeDtypeStruct((TAPS, channels), BF16),
            jax.ShapeDtypeStruct((TAPS, channels), BF16),
            jax.ShapeDtypeStruct((3, TAPS, channels), BF16),
            jax.ShapeDtypeStruct((TAPS, channels), F32),
        ],
        scratch_shapes=[
            pltpu.VMEM((3 * TAPS, LANES), BF16),
            pltpu.VMEM((3, own, LANES), F32),
            pltpu.VMEM((blocks, TAPS, LANES), F32),
            pltpu.VMEM((TAPS, 1), F32),
        ],
        compiler_params=pltpu.CompilerParams(**PARAMS),
        cost_estimate=pl.CostEstimate(flops=4 * 10**9, bytes_accessed=12 * 10**6, transcendentals=0),
    )(e_ext, q, k, v, g, x, x, r, gain, short, table)


def run_terms(dg, da, du, u, w, x, r):
    channels = x.shape[1]
    return pl.pallas_call(
        terms_kernel,
        grid=(channels // LANES,),
        in_specs=[
            tall(TAPS), BRANCH_SPEC, tall(TAPS), tall(TAPS + EDGE), tall(2 * TAPS), tall(TAPS),
            whole((TAPS, 1)),
        ],
        out_specs=[tall(1), tall(24), GROUP_SPEC],
        out_shape=[
            jax.ShapeDtypeStruct((1, channels), F32),
            jax.ShapeDtypeStruct((24, channels), F32),
            jax.ShapeDtypeStruct((channels // CH_GROUP, 2 * TAPS), F32),
        ],
        compiler_params=pltpu.CompilerParams(**PARAMS),
        cost_estimate=pl.CostEstimate(flops=4 * 10**9, bytes_accessed=8 * 10**6, transcendentals=0),
    )(dg, da, du, u, w, x, r)


def greet(me, count):
    barrier = pltpu.get_barrier_semaphore()

    def signal(d, carry):
        pl.semaphore_signal(barrier, inc=1, device_id={"fsdp": lax.rem(me + d, count)})
        return carry

    lax.fori_loop(1, count, signal, 0)
    pl.semaphore_wait(barrier, count - 1)


def start_kernel(
    count, flat_ref, x_ref, e_ref, every_ref, xe_ref, ee_ref, send, recv, halo_send, halo_recv
):
    me = lax.axis_index("fsdp")
    rows = x_ref.shape[0]
    halos = (
        (x_ref, 0, rows, xe_ref, EDGE, 1),
        (e_ref, 0, rows, ee_ref, rows, -1),
        (x_ref, 0, rows, xe_ref, EDGE + 2 * rows, -1),
        (x_ref, rows - EDGE, EDGE, xe_ref, 0, 2),
        (x_ref, 0, EDGE, xe_ref, EDGE + 3 * rows, -2),
        (e_ref, 0, EDGE, ee_ref, 2 * rows, -2),
    )

    def halo(i, target):
        source, first, size, landing, place, _ = halos[i]
        return pltpu.make_async_remote_copy(
            src_ref=source.at[pl.ds(first, size)],
            dst_ref=landing.at[pl.ds(place, size)],
            send_sem=halo_send.at[i],
            recv_sem=halo_recv.at[i],
            device_id={"fsdp": target},
        )

    def share(d):
        return pltpu.make_async_remote_copy(
            src_ref=flat_ref,
            dst_ref=every_ref.at[me],
            send_sem=send.at[d],
            recv_sem=recv.at[d],
            device_id={"fsdp": lax.rem(me + d, count)},
        )

    def sends(steps):
        return (me + steps >= 0) & (me + steps < count)

    greet(me, count)

    def begin(d, carry):
        share(d).start()
        return carry

    lax.fori_loop(1, count, begin, 0)
    for i, item in enumerate(halos):

        @pl.when(sends(item[5]))
        def _(i=i, steps=item[5]):
            halo(i, me + steps).start()

    every_ref[me] = flat_ref[...]
    xe_ref[EDGE + rows : EDGE + 2 * rows] = x_ref[...]
    ee_ref[:rows] = e_ref[...]
    for i, (_, _, size, landing, place, steps) in enumerate(halos):

        @pl.when(sends(-steps))
        def _(i=i, steps=steps):
            halo(i, me - steps).wait_recv()

        @pl.when(jnp.logical_not(sends(-steps)))
        def _(size=size, landing=landing, place=place):
            landing[place : place + size] = jnp.zeros((size, landing.shape[1]), landing.dtype)

        @pl.when(sends(steps))
        def _(i=i, steps=steps):
            halo(i, me + steps).wait_send()

    def finish(d, carry):
        share(d).wait()
        return carry

    lax.fori_loop(1, count, finish, 0)


def scatter_kernel(count, packed_ref, out_ref, landed, send, recv):
    me = lax.axis_index("fsdp")

    def share(d):
        peer = lax.rem(me + d, count)
        return pltpu.make_async_remote_copy(
            src_ref=packed_ref.at[peer],
            dst_ref=landed.at[d],
            send_sem=send.at[d],
            recv_sem=recv.at[d],
            device_id={"fsdp": peer},
        )

    greet(me, count)

    def begin(d, carry):
        share(d).start()
        return carry

    lax.fori_loop(1, count, begin, 0)
    out_ref[...] = packed_ref[me]

    def finish(d, carry):
        share(d).wait()
        out_ref[...] += landed[d]
        return carry

    lax.fori_loop(1, count, finish, 0)


def run_start(flat, x, e, shards):
    rows, channels = x.shape
    vmem = pl.BlockSpec(memory_space=pltpu.VMEM)
    dma = pltpu.SemaphoreType.DMA
    return pl.pallas_call(
        lambda *refs: start_kernel(shards, *refs),
        in_specs=[vmem] * 3,
        out_specs=[vmem] * 3,
        out_shape=[
            jax.ShapeDtypeStruct((shards,) + flat.shape, F32),
            jax.ShapeDtypeStruct((3 * rows + 2 * EDGE, channels), BF16),
            jax.ShapeDtypeStruct((2 * rows + EDGE, channels), BF16),
        ],
        scratch_shapes=[dma((shards,)), dma((shards,)), dma((6,)), dma((6,))],
        compiler_params=pltpu.CompilerParams(collective_id=0, has_side_effects=True, **PARAMS),
    )(flat, x, e)


def run_scatter(packed):
    shards = packed.shape[0]
    vmem = pl.BlockSpec(memory_space=pltpu.VMEM)
    dma = pltpu.SemaphoreType.DMA
    return pl.pallas_call(
        lambda *refs: scatter_kernel(shards, *refs),
        in_specs=[vmem],
        out_specs=vmem,
        out_shape=jax.ShapeDtypeStruct(packed.shape[1:], F32),
        scratch_shapes=[pltpu.VMEM(packed.shape, F32), dma((shards,)), dma((shards,))],
        compiler_params=pltpu.CompilerParams(collective_id=1, has_side_effects=True, **PARAMS),
    )(packed)


def shifted(value, steps):
    count = lax.axis_size("fsdp")
    initial, last = (max(0, -steps), min(count, count - steps))
    return lax.ppermute(value, "fsdp", [(source, source + steps) for source in range(initial, last)])


def crossed(value, steps):
    sections, count = lax.axis_size("section"), lax.axis_size("fsdp")
    pairs = [
        (s * count + f, ((s - 1) % sections) * count + f - steps)
        for s in range(sections)
        for f in range(steps, count)
    ]
    return lax.ppermute(value, ("section", "fsdp"), pairs)


def on_device(
    inputs, top_grad, gains, short_filters, medium_filters, lower_gain, lower_short, lower_medium
):
    shards = lax.axis_size("fsdp")
    last_section = lax.axis_index("section") == lax.axis_size("section") - 1
    chunk = gains.shape[1]
    channels = chunk * shards
    flat = jnp.stack(
        [
            jnp.concatenate([gains.reshape(-1), short_filters.reshape(-1), medium_filters.reshape(-1)]),
            jnp.concatenate([lower_gain, lower_short.reshape(-1), lower_medium.reshape(-1)]),
        ]
    )
    x1, x2, e1 = inputs[0, 0], inputs[1, 0], top_grad[0]
    extent = flat.shape[1]
    room = -(-extent // 1024) * 1024
    flat = jnp.pad(flat, ((0, 0), (0, room - extent))).reshape(-1, LANES)
    every, x1_ext, e1_ext = run_start(flat, x1, e1, shards)
    every = every.reshape(shards, 2, room)[:, :, :extent]

    def layer_params(part):
        gain = part[:, :chunk].reshape(1, channels)
        short = jnp.transpose(
            part[:, chunk : 22 * chunk].reshape(shards, 3 * SHORT, chunk), (1, 0, 2)
        ).reshape(3 * SHORT, channels)
        medium = jnp.transpose(
            part[:, 22 * chunk :].reshape(shards, -1, TAPS // shards), (1, 0, 2)
        ).reshape(-1, TAPS)
        medium = medium.astype(BF16).astype(F32)
        short = jnp.pad(short, ((0, 3), (0, 0)))
        causal = jnp.pad(medium[:, ::-1], ((0, 0), (1, TAPS - 1)))
        anti = jnp.pad(medium, ((0, 0), (0, TAPS)))
        return gain, short, causal, anti

    upper = every[:, 0]
    params = (layer_params(upper), layer_params(jnp.where(last_section, every[:, 1], upper)))

    def extended(x):
        rows = x.shape[0]
        return jnp.concatenate(
            [
                shifted(x[rows - EDGE :], 2), shifted(x, 1), x, shifted(x, -1),
                shifted(x[:EDGE], -2),
            ]
        )

    def row_scale(x_ext):
        wide = x_ext.astype(F32)
        return lax.rsqrt(jnp.mean(wide * wide, axis=-1, keepdims=True) + NORM_EPS)

    def terms_of(x, r, ahead, back):
        return run_terms(back[1], back[2], back[3], ahead[3], ahead[4], x, r)

    x2_ext = extended(x2)
    r1_ext, r2_ext = row_scale(x1_ext), row_scale(x2_ext)
    own_rows = slice(TAPS + EDGE, 2 * TAPS + EDGE)
    r1, r2 = r1_ext[own_rows], r2_ext[own_rows]
    (gain1, short1, causal1, anti1), (gain2, short2, causal2, anti2) = params
    ahead1 = run_forward(x1_ext, r1_ext, gain1, short1, causal1)
    back1 = run_backward(
        e1_ext, ahead1[0], ahead1[1], ahead1[2], ahead1[5], x1, r1, gain1, short1, anti1
    )
    dx1 = back1[0]
    e2_ext = jnp.concatenate([crossed(dx1, 0), crossed(dx1, 1), crossed(dx1[:EDGE], 2)])
    ahead2 = run_forward(x2_ext, r2_ext, gain2, short2, causal2)
    terms1 = terms_of(x1, r1, ahead1, back1)
    back2 = run_backward(
        e2_ext, ahead2[0], ahead2[1], ahead2[2], ahead2[5], x2, r2, gain2, short2, anti2
    )
    terms2 = terms_of(x2, r2, ahead2, back2)
    keep = jnp.where(last_section, 0.0, 1.0)
    tg, ts, tm = [a + keep * b for a, b in zip(terms1, terms2)]
    ts = jnp.transpose(ts[: 3 * SHORT].reshape(3 * SHORT, shards, chunk), (1, 0, 2))
    tm = tm[:, 1 : TAPS + 1][:, ::-1]
    groups = tm.shape[0]
    tm = jnp.transpose(tm.reshape(groups, shards, TAPS // shards), (1, 0, 2))
    packed = jnp.concatenate(
        [tg.reshape(shards, chunk), ts.reshape(shards, -1), tm.reshape(shards, -1)], axis=1
    )
    factor = (x1.shape[0] * shards) ** (-0.5)
    width = packed.shape[1]
    room = -(-width // 1024) * 1024
    packed = jnp.pad(packed, ((0, 0), (0, room - width))).reshape(shards, -1, LANES)
    summed = run_scatter(packed).reshape(-1) * factor
    return (
        back2[0][None],
        summed[:chunk][None],
        summed[chunk : 22 * chunk].reshape(1, 3, SHORT, chunk),
        summed[22 * chunk : 30 * chunk].reshape(1, groups, TAPS // shards),
    )


def solution(mesh):
    in_specs = (
        P(None, "section", "fsdp", None),
        P("section", "fsdp", None),
        P("section", "fsdp"),
        P("section", None, None, "fsdp"),
        P("section", None, "fsdp"),
        P("fsdp"),
        P(None, None, "fsdp"),
        P(None, "fsdp"),
    )
    out_specs = (
        P("section", "fsdp", None),
        P("section", "fsdp"),
        P("section", None, None, "fsdp"),
        P("section", None, "fsdp"),
    )
    return jax.shard_map(
        on_device, mesh=mesh, in_specs=in_specs, out_specs=out_specs, check_vma=False
    )
```

```python
import jax
import jax.numpy as jnp
from jax import lax
from jax.experimental import pallas as pl
from jax.experimental.pallas import tpu as pltpu
from jax.sharding import PartitionSpec as P

TAPS = 128
SHORT = 7
CH_GROUP = 16
NORM_EPS = 1e-06
LANES = 128
PER = LANES // CH_GROUP
EDGE = 16
F32 = jnp.float32
BF16 = jnp.bfloat16
PARAMS = dict(vmem_limit_bytes=48 * 2**20)


def toeplitz(row, rows):
    wide = jnp.broadcast_to(row, (rows, 2 * TAPS))
    return pltpu.roll(wide, 0, 1, stride=1, stride_axis=0).astype(BF16)


def band(table_ref, signal_ref):
    head = signal_ref[: 2 * TAPS]
    tail = signal_ref[TAPS : 3 * TAPS]
    group = lax.broadcasted_iota(jnp.int32, (TAPS, LANES), 1) // CH_GROUP
    group_edge = lax.broadcasted_iota(jnp.int32, (EDGE, LANES), 1) // CH_GROUP
    main = jnp.zeros((TAPS, LANES), F32)
    edge = jnp.zeros((EDGE, LANES), F32)
    edges = []
    for g in range(PER):
        table = toeplitz(table_ref[g : g + 1, :], TAPS)
        edges.append(table[:EDGE])
        part = jnp.dot(table, head, preferred_element_type=F32)
        main = jnp.where(group == g, part, main)
    parts = jnp.dot(jnp.concatenate(edges, 0), tail, preferred_element_type=F32)
    for g in range(PER):
        edge = jnp.where(group_edge == g, parts[g * EDGE : (g + 1) * EDGE], edge)
    return main, edge


def forward_kernel(
    x_ref, r_ref, gain_ref, short_ref, table_ref, q_ref, k_ref, v_ref, u_ref, w_ref, g_ref, us, ws
):
    total = x_ref.shape[0]
    own = TAPS + EDGE
    us[...] = x_ref[...].astype(F32) * r_ref[...] * gain_ref[...]
    u_ref[...] = us[TAPS : TAPS + own]
    half = (2 * TAPS + EDGE) // 2
    for part in range(2):
        low = part * half
        acc = None
        for j in range(SHORT):
            add = short_ref[j : j + 1, :] * us[own + low - j : own + low - j + half]
            acc = add if acc is None else acc + add
        q_ref[low : low + half] = acc
    for low, size in ((0, TAPS), (TAPS, own)):
        keys, values = None, None
        for j in range(SHORT):
            rows = us[EDGE + low - j : EDGE + low - j + size]
            key = short_ref[SHORT + j : SHORT + j + 1, :] * rows
            value = short_ref[2 * SHORT + j : 2 * SHORT + j + 1, :] * rows
            keys = key if keys is None else keys + key
            values = value if values is None else values + value
        ws[low : low + size] = (keys * values).astype(BF16)
        if low:
            k_ref[...] = keys
            v_ref[...] = values
    ws[2 * TAPS + EDGE :] = jnp.zeros((TAPS - EDGE, LANES), BF16)
    w_ref[...] = ws[: 2 * TAPS]
    main, edge = band(table_ref, ws)
    g_ref[:TAPS] = main
    g_ref[TAPS:] = edge


def backward_kernel(
    e_ref, q_ref, k_ref, v_ref, g_ref, xf_ref, x_ref, r_ref, gain_ref, short_ref, table_ref,
    dx_ref, dg_ref, da_ref, du_ref, dgs, das, held, means,
):
    step = pl.program_id(0)
    steps = pl.num_programs(0)
    own = TAPS + EDGE
    dgs[: TAPS + own] = (e_ref[...].astype(F32) * q_ref[...]).astype(BF16)
    dgs[TAPS + own :] = jnp.zeros((TAPS - EDGE, LANES), BF16)
    dg_ref[...] = dgs[:TAPS]
    main, edge = band(table_ref, dgs)
    for low, size, dw in ((0, TAPS, main), (TAPS, EDGE, edge)):
        rows = slice(low, low + size)
        das[0, rows] = (e_ref[rows].astype(F32) * g_ref[rows]).astype(BF16).astype(F32)
        das[1, rows] = (dw * v_ref[rows]).astype(BF16).astype(F32)
        das[2, rows] = (dw * k_ref[rows]).astype(BF16).astype(F32)
    da_ref[...] = das[:, :TAPS].astype(BF16)
    acc = None
    for c in range(3):
        for j in range(SHORT):
            add = short_ref[SHORT * c + j : SHORT * c + j + 1, :] * das[c, j : j + TAPS]
            acc = add if acc is None else acc + add
    du_ref[...] = acc
    scaled = gain_ref[...] * acc
    part = jnp.sum(x_ref[...].astype(F32) * scaled, axis=1, keepdims=True)

    @pl.when(step == 0)
    def _():
        means[...] = jnp.zeros_like(means)

    means[...] += part
    held[step] = e_ref[:TAPS].astype(F32) + r_ref[...] * scaled

    @pl.when(step == steps - 1)
    def _():
        r = r_ref[...]
        factor = r * r * r * (means[...] * (1.0 / dx_ref.shape[1]))
        for b in range(dx_ref.shape[1] // LANES):
            lanes = slice(b * LANES, (b + 1) * LANES)
            dx_ref[:, lanes] = (held[b] - xf_ref[:, lanes].astype(F32) * factor).astype(BF16)


def terms_kernel(
    dg_ref, da_ref, du_ref, u_ref, w_ref, x_ref, r_ref, tg_ref, ts_ref, tm_ref
):
    tg_ref[...] = jnp.sum(du_ref[...] * x_ref[...].astype(F32) * r_ref[...], axis=0, keepdims=True)
    for c in range(3):
        grads = da_ref[c].astype(F32)
        for j in range(SHORT):
            row = SHORT * c + j
            ts_ref[row : row + 1, :] = jnp.sum(
                grads * u_ref[EDGE - j : EDGE - j + TAPS], axis=0, keepdims=True
            )
    ts_ref[3 * SHORT :, :] = jnp.zeros((3, LANES), F32)
    grads = dg_ref[...].astype(F32)
    mask = (
        lax.broadcasted_iota(jnp.int32, (1, PER, LANES), 2) // CH_GROUP
        == lax.broadcasted_iota(jnp.int32, (1, PER, LANES), 1)
    )
    spread = jnp.where(mask, jnp.broadcast_to(grads[:, None, :], (TAPS, PER, LANES)), 0.0)
    spread = spread.reshape(TAPS * PER, LANES).astype(BF16)
    lags = lax.dot_general(
        spread, w_ref[...], (((1,), (1,)), ((), ())), preferred_element_type=F32
    )
    total = lags[:PER]
    for t in range(1, TAPS):
        total = total + pltpu.roll(lags[t * PER : (t + 1) * PER], 2 * TAPS - t, 1)
    tm_ref[...] = total


def tall(rows, dtype=F32):
    return pl.BlockSpec((rows, LANES), lambda i: (0, i))


def whole(shape):
    return pl.BlockSpec(shape, lambda i: (0,) * len(shape))


GROUP_SPEC = pl.BlockSpec((PER, 2 * TAPS), lambda i: (i, 0))
BRANCH_SPEC = pl.BlockSpec((3, TAPS, LANES), lambda i: (0, 0, i))


def run_backward(e_ext, q, k, v, g, x, r, gain, short, table):
    channels = x.shape[1]
    own = TAPS + EDGE
    blocks = channels // LANES
    return pl.pallas_call(
        backward_kernel,
        grid=(blocks,),
        in_specs=[
            tall(TAPS + own), tall(TAPS + own), tall(own), tall(own), tall(own),
            whole((TAPS, channels)), tall(TAPS), whole((TAPS, 1)), tall(1), tall(24), GROUP_SPEC,
        ],
        out_specs=[whole((TAPS, channels)), tall(TAPS), BRANCH_SPEC, tall(TAPS)],
        out_shape=[
            jax.ShapeDtypeStruct((TAPS, channels), BF16),
            jax.ShapeDtypeStruct((TAPS, channels), BF16),
            jax.ShapeDtypeStruct((3, TAPS, channels), BF16),
            jax.ShapeDtypeStruct((TAPS, channels), F32),
        ],
        scratch_shapes=[
            pltpu.VMEM((3 * TAPS, LANES), BF16),
            pltpu.VMEM((3, own, LANES), F32),
            pltpu.VMEM((blocks, TAPS, LANES), F32),
            pltpu.VMEM((TAPS, 1), F32),
        ],
        compiler_params=pltpu.CompilerParams(**PARAMS),
        cost_estimate=pl.CostEstimate(flops=4 * 10**9, bytes_accessed=12 * 10**6, transcendentals=0),
    )(e_ext, q, k, v, g, x, x, r, gain, short, table)


def run_terms(dg, da, du, u, w, x, r):
    channels = x.shape[1]
    return pl.pallas_call(
        terms_kernel,
        grid=(channels // LANES,),
        in_specs=[
            tall(TAPS), BRANCH_SPEC, tall(TAPS), tall(TAPS + EDGE), tall(2 * TAPS), tall(TAPS),
            whole((TAPS, 1)),
        ],
        out_specs=[tall(1), tall(24), GROUP_SPEC],
        out_shape=[
            jax.ShapeDtypeStruct((1, channels), F32),
            jax.ShapeDtypeStruct((24, channels), F32),
            jax.ShapeDtypeStruct((channels // CH_GROUP, 2 * TAPS), F32),
        ],
        compiler_params=pltpu.CompilerParams(**PARAMS),
        cost_estimate=pl.CostEstimate(flops=4 * 10**9, bytes_accessed=8 * 10**6, transcendentals=0),
    )(dg, da, du, u, w, x, r)


def greet(me, count):
    barrier = pltpu.get_barrier_semaphore()

    def signal(d, carry):
        pl.semaphore_signal(barrier, inc=1, device_id={"fsdp": lax.rem(me + d, count)})
        return carry

    lax.fori_loop(1, count, signal, 0)
    pl.semaphore_wait(barrier, count - 1)


def start_kernel(
    count, flat_ref, x_ref, every_ref, xe_ref, send, recv, halo_send, halo_recv
):
    me = lax.axis_index("fsdp")
    rows = x_ref.shape[0]
    halos = (
        (x_ref, 0, rows, xe_ref, EDGE, 1),
        (x_ref, 0, rows, xe_ref, EDGE + 2 * rows, -1),
        (x_ref, rows - EDGE, EDGE, xe_ref, 0, 2),
        (x_ref, 0, EDGE, xe_ref, EDGE + 3 * rows, -2),
    )

    def halo(i, target):
        source, first, size, landing, place, _ = halos[i]
        return pltpu.make_async_remote_copy(
            src_ref=source.at[pl.ds(first, size)],
            dst_ref=landing.at[pl.ds(place, size)],
            send_sem=halo_send.at[i],
            recv_sem=halo_recv.at[i],
            device_id={"fsdp": target},
        )

    def share(d):
        return pltpu.make_async_remote_copy(
            src_ref=flat_ref,
            dst_ref=every_ref.at[me],
            send_sem=send.at[d],
            recv_sem=recv.at[d],
            device_id={"fsdp": lax.rem(me + d, count)},
        )

    def sends(steps):
        return (me + steps >= 0) & (me + steps < count)

    greet(me, count)

    def begin(d, carry):
        share(d).start()
        return carry

    lax.fori_loop(1, count, begin, 0)
    for i, item in enumerate(halos):

        @pl.when(sends(item[5]))
        def _(i=i, steps=item[5]):
            halo(i, me + steps).start()

    every_ref[me] = flat_ref[...]
    xe_ref[EDGE + rows : EDGE + 2 * rows] = x_ref[...]
    for i, (_, _, size, landing, place, steps) in enumerate(halos):

        @pl.when(sends(-steps))
        def _(i=i, steps=steps):
            halo(i, me - steps).wait_recv()

        @pl.when(jnp.logical_not(sends(-steps)))
        def _(size=size, landing=landing, place=place):
            landing[place : place + size] = jnp.zeros((size, landing.shape[1]), landing.dtype)

        @pl.when(sends(steps))
        def _(i=i, steps=steps):
            halo(i, me + steps).wait_send()

    def finish(d, carry):
        share(d).wait()
        return carry

    lax.fori_loop(1, count, finish, 0)


def scatter_kernel(count, packed_ref, out_ref, landed, send, recv):
    me = lax.axis_index("fsdp")

    def share(d):
        peer = lax.rem(me + d, count)
        return pltpu.make_async_remote_copy(
            src_ref=packed_ref.at[peer],
            dst_ref=landed.at[d],
            send_sem=send.at[d],
            recv_sem=recv.at[d],
            device_id={"fsdp": peer},
        )

    greet(me, count)

    def begin(d, carry):
        share(d).start()
        return carry

    lax.fori_loop(1, count, begin, 0)
    out_ref[...] = packed_ref[me]

    def finish(d, carry):
        share(d).wait()
        out_ref[...] += landed[d]
        return carry

    lax.fori_loop(1, count, finish, 0)


def run_start(flat, x, shards):
    rows, channels = x.shape
    vmem = pl.BlockSpec(memory_space=pltpu.VMEM)
    dma = pltpu.SemaphoreType.DMA
    return pl.pallas_call(
        lambda *refs: start_kernel(shards, *refs),
        in_specs=[vmem] * 2,
        out_specs=[vmem] * 2,
        out_shape=[
            jax.ShapeDtypeStruct((shards,) + flat.shape, F32),
            jax.ShapeDtypeStruct((3 * rows + 2 * EDGE, channels), BF16),
        ],
        scratch_shapes=[dma((shards,)), dma((shards,)), dma((4,)), dma((4,))],
        compiler_params=pltpu.CompilerParams(collective_id=0, has_side_effects=True, **PARAMS),
    )(flat, x)


def run_scatter(packed):
    shards = packed.shape[0]
    vmem = pl.BlockSpec(memory_space=pltpu.VMEM)
    dma = pltpu.SemaphoreType.DMA
    return pl.pallas_call(
        lambda *refs: scatter_kernel(shards, *refs),
        in_specs=[vmem],
        out_specs=vmem,
        out_shape=jax.ShapeDtypeStruct(packed.shape[1:], F32),
        scratch_shapes=[pltpu.VMEM(packed.shape, F32), dma((shards,)), dma((shards,))],
        compiler_params=pltpu.CompilerParams(collective_id=1, has_side_effects=True, **PARAMS),
    )(packed)


def exchange_parts(sections, count, moves, owned, zeros, send, recv, local):
    section, me = lax.axis_index("section"), lax.axis_index("fsdp")

    def device(dsection, steps):
        return {"section": lax.rem(section + dsection + sections, sections), "fsdp": me + steps}

    def copy(i):
        source, first, size, landing, place, dsection, steps = moves[i]
        return pltpu.make_async_remote_copy(
            src_ref=source.at[pl.ds(first, size)],
            dst_ref=landing.at[pl.ds(place, size)],
            send_sem=send.at[i],
            recv_sem=recv.at[i],
            device_id=device(dsection, steps),
        )

    def keep(i):
        source, landing, place = owned[i]
        return pltpu.make_async_copy(
            source, landing.at[pl.ds(place, source.shape[0])], local.at[i]
        )

    def inside(steps):
        return (me + steps >= 0) & (me + steps < count)

    routes = sorted({move[5:] for move in moves})

    def begin():
        barrier = pltpu.get_barrier_semaphore()
        for dsection, steps in routes:

            @pl.when(inside(-steps))
            def _(dsection=dsection, steps=steps):
                pl.semaphore_signal(barrier, inc=1, device_id=device(-dsection, -steps))

        pl.semaphore_wait(barrier, sum(inside(steps).astype(jnp.int32) for _, steps in routes))
        for i, move in enumerate(moves):

            @pl.when(inside(move[6]))
            def _(i=i):
                copy(i).start()

        for i in range(len(owned)):
            keep(i).start()
        zeros[...] = jnp.zeros_like(zeros)
        for i, (_, _, size, landing, place, _, steps) in enumerate(moves):

            @pl.when(jnp.logical_not(inside(-steps)))
            def _(size=size, landing=landing, place=place):
                clear = pltpu.make_async_copy(
                    zeros.at[pl.ds(0, size)],
                    landing.at[pl.ds(place, size)],
                    local.at[len(owned)],
                )
                clear.start()
                clear.wait()

    def finish():
        for i, move in enumerate(moves):

            @pl.when(inside(-move[6]))
            def _(i=i):
                copy(i).wait_recv()

            @pl.when(inside(move[6]))
            def _(i=i):
                copy(i).wait_send()

        for i in range(len(owned)):
            keep(i).wait()

    return begin, finish


def around(begin, finish, body):
    step = pl.program_id(0)
    pl.when(step == 0)(begin)
    body()
    pl.when(step == pl.num_programs(0) - 1)(finish)


def first_forward_kernel(
    sections, count, x_ref, r_ref, gain_ref, short_ref, table_ref, y_ref, e_ref,
    q_ref, k_ref, v_ref, u_ref, w_ref, g_ref, ye_ref, ee_ref, us, ws, zeros, send, recv, local,
):
    rows = y_ref.shape[0]
    moves = (
        (e_ref, 0, rows, ee_ref, rows, 0, -1),
        (e_ref, 0, EDGE, ee_ref, 2 * rows, 0, -2),
        (y_ref, 0, rows, ye_ref, EDGE, 0, 1),
        (y_ref, 0, rows, ye_ref, EDGE + 2 * rows, 0, -1),
        (y_ref, rows - EDGE, EDGE, ye_ref, 0, 0, 2),
        (y_ref, 0, EDGE, ye_ref, EDGE + 3 * rows, 0, -2),
    )
    owned = ((e_ref, ee_ref, 0), (y_ref, ye_ref, EDGE + rows))
    begin, finish = exchange_parts(sections, count, moves, owned, zeros, send, recv, local)
    around(
        begin,
        finish,
        lambda: forward_kernel(
            x_ref, r_ref, gain_ref, short_ref, table_ref,
            q_ref, k_ref, v_ref, u_ref, w_ref, g_ref, us, ws,
        ),
    )


def middle_kernel(sections, count, *refs):
    forward_in, terms_in, d_ref = refs[:5], refs[5:12], refs[12]
    forward_out, terms_out, ee_ref = refs[13:19], refs[19:22], refs[22]
    us, ws, zeros, send, recv, local = refs[23:]
    rows = d_ref.shape[0]
    moves = (
        (d_ref, 0, rows, ee_ref, 0, -1, 0),
        (d_ref, 0, rows, ee_ref, rows, -1, -1),
        (d_ref, 0, EDGE, ee_ref, 2 * rows, -1, -2),
    )
    begin, finish = exchange_parts(sections, count, moves, (), zeros, send, recv, local)

    def body():
        forward_kernel(*forward_in, *forward_out, us, ws)
        terms_kernel(*terms_in, *terms_out)

    around(begin, finish, body)


def forward_specs(total, channels):
    own = TAPS + EDGE
    shapes = [(TAPS + own, F32), (own, F32), (own, F32), (own, F32), (2 * TAPS, BF16), (own, F32)]
    return (
        [tall(total), whole((total, 1)), tall(1), tall(24), GROUP_SPEC],
        [tall(rows) for rows, _ in shapes],
        [jax.ShapeDtypeStruct((rows, channels), kind) for rows, kind in shapes],
        [pltpu.VMEM((total, LANES), F32), pltpu.VMEM((3 * TAPS, LANES), BF16)],
    )


def terms_specs(channels):
    return (
        [
            tall(TAPS), BRANCH_SPEC, tall(TAPS), tall(TAPS + EDGE), tall(2 * TAPS), tall(TAPS),
            whole((TAPS, 1)),
        ],
        [tall(1), tall(24), GROUP_SPEC],
        [
            jax.ShapeDtypeStruct((1, channels), F32),
            jax.ShapeDtypeStruct((24, channels), F32),
            jax.ShapeDtypeStruct((channels // CH_GROUP, 2 * TAPS), F32),
        ],
    )


def exchange_scratch(moves, owned, rows, channels):
    dma = pltpu.SemaphoreType.DMA
    return [pltpu.VMEM((rows, channels), BF16), dma((moves,)), dma((moves,)), dma((owned + 1,))]


def run_first_forward(forward_args, y, e, sections, count):
    rows, channels = y.shape
    ins, outs, shapes, scratch = forward_specs(forward_args[0].shape[0], channels)
    remote = pl.BlockSpec(memory_space=pl.ANY)
    return pl.pallas_call(
        lambda *refs: first_forward_kernel(sections, count, *refs),
        grid=(channels // LANES,),
        in_specs=ins + [remote] * 2,
        out_specs=outs + [remote] * 2,
        out_shape=shapes
        + [
            jax.ShapeDtypeStruct((3 * rows + 2 * EDGE, channels), BF16),
            jax.ShapeDtypeStruct((2 * rows + EDGE, channels), BF16),
        ],
        scratch_shapes=scratch + exchange_scratch(6, 2, rows, channels),
        compiler_params=pltpu.CompilerParams(collective_id=2, has_side_effects=True, **PARAMS),
    )(*forward_args, y, e)


def run_middle(forward_args, terms_args, d, sections, count):
    rows, channels = d.shape
    ins, outs, shapes, scratch = forward_specs(forward_args[0].shape[0], channels)
    more_ins, more_outs, more_shapes = terms_specs(channels)
    remote = pl.BlockSpec(memory_space=pl.ANY)
    return pl.pallas_call(
        lambda *refs: middle_kernel(sections, count, *refs),
        grid=(channels // LANES,),
        in_specs=ins + more_ins + [remote],
        out_specs=outs + more_outs + [remote],
        out_shape=shapes
        + more_shapes
        + [jax.ShapeDtypeStruct((2 * rows + EDGE, channels), BF16)],
        scratch_shapes=scratch + exchange_scratch(3, 0, rows, channels),
        compiler_params=pltpu.CompilerParams(collective_id=3, has_side_effects=True, **PARAMS),
    )(*forward_args, *terms_args, d)


def on_device(
    inputs, top_grad, gains, short_filters, medium_filters, lower_gain, lower_short, lower_medium
):
    shards = lax.axis_size("fsdp")
    last_section = lax.axis_index("section") == lax.axis_size("section") - 1
    chunk = gains.shape[1]
    channels = chunk * shards
    flat = jnp.stack(
        [
            jnp.concatenate([gains.reshape(-1), short_filters.reshape(-1), medium_filters.reshape(-1)]),
            jnp.concatenate([lower_gain, lower_short.reshape(-1), lower_medium.reshape(-1)]),
        ]
    )
    x1, x2, e1 = inputs[0, 0], inputs[1, 0], top_grad[0]
    extent = flat.shape[1]
    room = -(-extent // 1024) * 1024
    flat = jnp.pad(flat, ((0, 0), (0, room - extent))).reshape(-1, LANES)
    every, x1_ext = run_start(flat, x1, shards)
    every = every.reshape(shards, 2, room)[:, :, :extent]

    def layer_params(part):
        gain = part[:, :chunk].reshape(1, channels)
        short = jnp.transpose(
            part[:, chunk : 22 * chunk].reshape(shards, 3 * SHORT, chunk), (1, 0, 2)
        ).reshape(3 * SHORT, channels)
        medium = jnp.transpose(
            part[:, 22 * chunk :].reshape(shards, -1, TAPS // shards), (1, 0, 2)
        ).reshape(-1, TAPS)
        medium = medium.astype(BF16).astype(F32)
        short = jnp.pad(short, ((0, 3), (0, 0)))
        causal = jnp.pad(medium[:, ::-1], ((0, 0), (1, TAPS - 1)))
        anti = jnp.pad(medium, ((0, 0), (0, TAPS)))
        return gain, short, causal, anti

    upper = every[:, 0]
    params = (layer_params(upper), layer_params(jnp.where(last_section, every[:, 1], upper)))

    def row_scale(x_ext):
        wide = x_ext.astype(F32)
        return lax.rsqrt(jnp.mean(wide * wide, axis=-1, keepdims=True) + NORM_EPS)

    own_rows = slice(TAPS + EDGE, 2 * TAPS + EDGE)
    (gain1, short1, causal1, anti1), (gain2, short2, causal2, anti2) = params
    sections = lax.axis_size("section")
    r1_ext = row_scale(x1_ext)
    r1 = r1_ext[own_rows]
    *ahead1, x2_ext, e1_ext = run_first_forward(
        (x1_ext, r1_ext, gain1, short1, causal1), x2, e1, sections, shards
    )
    r2_ext = row_scale(x2_ext)
    r2 = r2_ext[own_rows]
    dx1, *back1 = run_backward(
        e1_ext, ahead1[0], ahead1[1], ahead1[2], ahead1[5], x1, r1, gain1, short1, anti1
    )
    middle = run_middle(
        (x2_ext, r2_ext, gain2, short2, causal2),
        (*back1, ahead1[3], ahead1[4], x1, r1),
        dx1,
        sections,
        shards,
    )
    ahead2, terms1, e2_ext = middle[:6], middle[6:9], middle[9]
    dx2, *back2 = run_backward(
        e2_ext, ahead2[0], ahead2[1], ahead2[2], ahead2[5], x2, r2, gain2, short2, anti2
    )
    terms2 = run_terms(*back2, ahead2[3], ahead2[4], x2, r2)
    keep = jnp.where(last_section, 0.0, 1.0)
    tg, ts, tm = [a + keep * b for a, b in zip(terms1, terms2)]
    ts = jnp.transpose(ts[: 3 * SHORT].reshape(3 * SHORT, shards, chunk), (1, 0, 2))
    tm = tm[:, 1 : TAPS + 1][:, ::-1]
    groups = tm.shape[0]
    tm = jnp.transpose(tm.reshape(groups, shards, TAPS // shards), (1, 0, 2))
    packed = jnp.concatenate(
        [tg.reshape(shards, chunk), ts.reshape(shards, -1), tm.reshape(shards, -1)], axis=1
    )
    factor = (x1.shape[0] * shards) ** (-0.5)
    width = packed.shape[1]
    room = -(-width // 1024) * 1024
    packed = jnp.pad(packed, ((0, 0), (0, room - width))).reshape(shards, -1, LANES)
    summed = run_scatter(packed).reshape(-1) * factor
    return (
        dx2[None],
        summed[:chunk][None],
        summed[chunk : 22 * chunk].reshape(1, 3, SHORT, chunk),
        summed[22 * chunk : 30 * chunk].reshape(1, groups, TAPS // shards),
    )


def solution(mesh):
    in_specs = (
        P(None, "section", "fsdp", None),
        P("section", "fsdp", None),
        P("section", "fsdp"),
        P("section", None, None, "fsdp"),
        P("section", None, "fsdp"),
        P("fsdp"),
        P(None, None, "fsdp"),
        P(None, "fsdp"),
    )
    out_specs = (
        P("section", "fsdp", None),
        P("section", "fsdp"),
        P("section", None, None, "fsdp"),
        P("section", None, "fsdp"),
    )
    return jax.shard_map(
        on_device, mesh=mesh, in_specs=in_specs, out_specs=out_specs, check_vma=False
    )
```

```python
import jax
import jax.numpy as jnp
from jax import lax
from jax.experimental import pallas as pl
from jax.experimental.pallas import tpu as pltpu
from jax.sharding import PartitionSpec as P

TAPS = 128
SHORT = 7
CH_GROUP = 16
NORM_EPS = 1e-06
LANES = 128
PER = LANES // CH_GROUP
EDGE = 16
F32 = jnp.float32
BF16 = jnp.bfloat16
PARAMS = dict(vmem_limit_bytes=48 * 2**20)


def toeplitz(row, rows):
    wide = jnp.broadcast_to(row, (rows, 2 * TAPS))
    return pltpu.roll(wide, 0, 1, stride=1, stride_axis=0).astype(BF16)


def band(table_ref, signal_ref):
    head = signal_ref[: 2 * TAPS]
    tail = signal_ref[TAPS : 3 * TAPS]
    group = lax.broadcasted_iota(jnp.int32, (TAPS, LANES), 1) // CH_GROUP
    group_edge = lax.broadcasted_iota(jnp.int32, (EDGE, LANES), 1) // CH_GROUP
    main = jnp.zeros((TAPS, LANES), F32)
    edge = jnp.zeros((EDGE, LANES), F32)
    edges = []
    for g in range(PER):
        table = toeplitz(table_ref[g : g + 1, :], TAPS)
        edges.append(table[:EDGE])
        part = jnp.dot(table, head, preferred_element_type=F32)
        main = jnp.where(group == g, part, main)
    parts = jnp.dot(jnp.concatenate(edges, 0), tail, preferred_element_type=F32)
    for g in range(PER):
        edge = jnp.where(group_edge == g, parts[g * EDGE : (g + 1) * EDGE], edge)
    return main, edge


def forward_kernel(
    x_ref, r_ref, gain_ref, short_ref, table_ref, q_ref, k_ref, v_ref, u_ref, w_ref, g_ref, us, ws
):
    total = x_ref.shape[0]
    own = TAPS + EDGE
    us[...] = x_ref[...].astype(F32) * r_ref[...] * gain_ref[...]
    u_ref[...] = us[TAPS : TAPS + own]
    half = (2 * TAPS + EDGE) // 2
    for part in range(2):
        low = part * half
        acc = None
        for j in range(SHORT):
            add = short_ref[j : j + 1, :] * us[own + low - j : own + low - j + half]
            acc = add if acc is None else acc + add
        q_ref[low : low + half] = acc
    for low, size in ((0, TAPS), (TAPS, own)):
        keys, values = None, None
        for j in range(SHORT):
            rows = us[EDGE + low - j : EDGE + low - j + size]
            key = short_ref[SHORT + j : SHORT + j + 1, :] * rows
            value = short_ref[2 * SHORT + j : 2 * SHORT + j + 1, :] * rows
            keys = key if keys is None else keys + key
            values = value if values is None else values + value
        ws[low : low + size] = (keys * values).astype(BF16)
        if low:
            k_ref[...] = keys
            v_ref[...] = values
    ws[2 * TAPS + EDGE :] = jnp.zeros((TAPS - EDGE, LANES), BF16)
    w_ref[...] = ws[: 2 * TAPS]
    main, edge = band(table_ref, ws)
    g_ref[:TAPS] = main
    g_ref[TAPS:] = edge


def backward_kernel(
    e_ref, q_ref, k_ref, v_ref, g_ref, xf_ref, x_ref, r_ref, gain_ref, short_ref, table_ref,
    dx_ref, dg_ref, da_ref, du_ref, dgs, das, held, means,
):
    step = pl.program_id(0)
    steps = pl.num_programs(0)
    own = TAPS + EDGE
    dgs[: TAPS + own] = (e_ref[...].astype(F32) * q_ref[...]).astype(BF16)
    dgs[TAPS + own :] = jnp.zeros((TAPS - EDGE, LANES), BF16)
    dg_ref[...] = dgs[:TAPS]
    main, edge = band(table_ref, dgs)
    for low, size, dw in ((0, TAPS, main), (TAPS, EDGE, edge)):
        rows = slice(low, low + size)
        das[0, rows] = (e_ref[rows].astype(F32) * g_ref[rows]).astype(BF16).astype(F32)
        das[1, rows] = (dw * v_ref[rows]).astype(BF16).astype(F32)
        das[2, rows] = (dw * k_ref[rows]).astype(BF16).astype(F32)
    da_ref[...] = das[:, :TAPS].astype(BF16)
    acc = None
    for c in range(3):
        for j in range(SHORT):
            add = short_ref[SHORT * c + j : SHORT * c + j + 1, :] * das[c, j : j + TAPS]
            acc = add if acc is None else acc + add
    du_ref[...] = acc
    scaled = gain_ref[...] * acc
    part = jnp.sum(x_ref[...].astype(F32) * scaled, axis=1, keepdims=True)

    @pl.when(step == 0)
    def _():
        means[...] = jnp.zeros_like(means)

    means[...] += part
    held[step] = e_ref[:TAPS].astype(F32) + r_ref[...] * scaled

    @pl.when(step == steps - 1)
    def _():
        r = r_ref[...]
        factor = r * r * r * (means[...] * (1.0 / dx_ref.shape[1]))
        for b in range(dx_ref.shape[1] // LANES):
            lanes = slice(b * LANES, (b + 1) * LANES)
            dx_ref[:, lanes] = (held[b] - xf_ref[:, lanes].astype(F32) * factor).astype(BF16)


def terms_kernel(
    dg_ref, da_ref, du_ref, u_ref, w_ref, x_ref, r_ref, tg_ref, ts_ref, tm_ref
):
    tg_ref[...] = jnp.sum(du_ref[...] * x_ref[...].astype(F32) * r_ref[...], axis=0, keepdims=True)
    for c in range(3):
        grads = da_ref[c].astype(F32)
        for j in range(SHORT):
            row = SHORT * c + j
            ts_ref[row : row + 1, :] = jnp.sum(
                grads * u_ref[EDGE - j : EDGE - j + TAPS], axis=0, keepdims=True
            )
    ts_ref[3 * SHORT :, :] = jnp.zeros((3, LANES), F32)
    grads = dg_ref[...].astype(F32)
    mask = (
        lax.broadcasted_iota(jnp.int32, (1, PER, LANES), 2) // CH_GROUP
        == lax.broadcasted_iota(jnp.int32, (1, PER, LANES), 1)
    )
    spread = jnp.where(mask, jnp.broadcast_to(grads[:, None, :], (TAPS, PER, LANES)), 0.0)
    spread = spread.reshape(TAPS * PER, LANES).astype(BF16)
    lags = lax.dot_general(
        spread, w_ref[...], (((1,), (1,)), ((), ())), preferred_element_type=F32
    )
    total = lags[:PER]
    for t in range(1, TAPS):
        total = total + pltpu.roll(lags[t * PER : (t + 1) * PER], 2 * TAPS - t, 1)
    tm_ref[...] = total


def tall(rows, dtype=F32):
    return pl.BlockSpec((rows, LANES), lambda i: (0, i))


def whole(shape):
    return pl.BlockSpec(shape, lambda i: (0,) * len(shape))


GROUP_SPEC = pl.BlockSpec((PER, 2 * TAPS), lambda i: (i, 0))
BRANCH_SPEC = pl.BlockSpec((3, TAPS, LANES), lambda i: (0, 0, i))


def run_backward(e_ext, q, k, v, g, x, r, gain, short, table):
    channels = x.shape[1]
    own = TAPS + EDGE
    blocks = channels // LANES
    return pl.pallas_call(
        backward_kernel,
        grid=(blocks,),
        in_specs=[
            tall(TAPS + own), tall(TAPS + own), tall(own), tall(own), tall(own),
            whole((TAPS, channels)), tall(TAPS), whole((TAPS, 1)), tall(1), tall(24), GROUP_SPEC,
        ],
        out_specs=[whole((TAPS, channels)), tall(TAPS), BRANCH_SPEC, tall(TAPS)],
        out_shape=[
            jax.ShapeDtypeStruct((TAPS, channels), BF16),
            jax.ShapeDtypeStruct((TAPS, channels), BF16),
            jax.ShapeDtypeStruct((3, TAPS, channels), BF16),
            jax.ShapeDtypeStruct((TAPS, channels), F32),
        ],
        scratch_shapes=[
            pltpu.VMEM((3 * TAPS, LANES), BF16),
            pltpu.VMEM((3, own, LANES), F32),
            pltpu.VMEM((blocks, TAPS, LANES), F32),
            pltpu.VMEM((TAPS, 1), F32),
        ],
        compiler_params=pltpu.CompilerParams(**PARAMS),
        cost_estimate=pl.CostEstimate(flops=4 * 10**9, bytes_accessed=12 * 10**6, transcendentals=0),
    )(e_ext, q, k, v, g, x, x, r, gain, short, table)


def run_terms(dg, da, du, u, w, x, r):
    channels = x.shape[1]
    return pl.pallas_call(
        terms_kernel,
        grid=(channels // LANES,),
        in_specs=[
            tall(TAPS), BRANCH_SPEC, tall(TAPS), tall(TAPS + EDGE), tall(2 * TAPS), tall(TAPS),
            whole((TAPS, 1)),
        ],
        out_specs=[tall(1), tall(24), GROUP_SPEC],
        out_shape=[
            jax.ShapeDtypeStruct((1, channels), F32),
            jax.ShapeDtypeStruct((24, channels), F32),
            jax.ShapeDtypeStruct((channels // CH_GROUP, 2 * TAPS), F32),
        ],
        compiler_params=pltpu.CompilerParams(**PARAMS),
        cost_estimate=pl.CostEstimate(flops=4 * 10**9, bytes_accessed=8 * 10**6, transcendentals=0),
    )(dg, da, du, u, w, x, r)


def greet(me, count):
    barrier = pltpu.get_barrier_semaphore()

    def signal(d, carry):
        pl.semaphore_signal(barrier, inc=1, device_id={"fsdp": lax.rem(me + d, count)})
        return carry

    lax.fori_loop(1, count, signal, 0)
    pl.semaphore_wait(barrier, count - 1)


def start_kernel(
    count, flat_ref, x_ref, every_ref, xe_ref, send, recv, halo_send, halo_recv
):
    me = lax.axis_index("fsdp")
    rows = x_ref.shape[0]
    halos = (
        (x_ref, 0, rows, xe_ref, EDGE, 1),
        (x_ref, 0, rows, xe_ref, EDGE + 2 * rows, -1),
        (x_ref, rows - EDGE, EDGE, xe_ref, 0, 2),
        (x_ref, 0, EDGE, xe_ref, EDGE + 3 * rows, -2),
    )

    def halo(i, target):
        source, first, size, landing, place, _ = halos[i]
        return pltpu.make_async_remote_copy(
            src_ref=source.at[pl.ds(first, size)],
            dst_ref=landing.at[pl.ds(place, size)],
            send_sem=halo_send.at[i],
            recv_sem=halo_recv.at[i],
            device_id={"fsdp": target},
        )

    def share(d):
        return pltpu.make_async_remote_copy(
            src_ref=flat_ref,
            dst_ref=every_ref.at[me],
            send_sem=send.at[d],
            recv_sem=recv.at[d],
            device_id={"fsdp": lax.rem(me + d, count)},
        )

    def sends(steps):
        return (me + steps >= 0) & (me + steps < count)

    greet(me, count)

    def begin(d, carry):
        share(d).start()
        return carry

    lax.fori_loop(1, count, begin, 0)
    for i, item in enumerate(halos):

        @pl.when(sends(item[5]))
        def _(i=i, steps=item[5]):
            halo(i, me + steps).start()

    every_ref[me] = flat_ref[...]
    xe_ref[EDGE + rows : EDGE + 2 * rows] = x_ref[...]
    for i, (_, _, size, landing, place, steps) in enumerate(halos):

        @pl.when(sends(-steps))
        def _(i=i, steps=steps):
            halo(i, me - steps).wait_recv()

        @pl.when(jnp.logical_not(sends(-steps)))
        def _(size=size, landing=landing, place=place):
            landing[place : place + size] = jnp.zeros((size, landing.shape[1]), landing.dtype)

        @pl.when(sends(steps))
        def _(i=i, steps=steps):
            halo(i, me + steps).wait_send()

    def finish(d, carry):
        share(d).wait()
        return carry

    lax.fori_loop(1, count, finish, 0)


def scatter_kernel(count, packed_ref, out_ref, landed, send, recv):
    me = lax.axis_index("fsdp")

    def share(d):
        peer = lax.rem(me + d, count)
        return pltpu.make_async_remote_copy(
            src_ref=packed_ref.at[peer],
            dst_ref=landed.at[d],
            send_sem=send.at[d],
            recv_sem=recv.at[d],
            device_id={"fsdp": peer},
        )

    greet(me, count)

    def begin(d, carry):
        share(d).start()
        return carry

    lax.fori_loop(1, count, begin, 0)
    out_ref[...] = packed_ref[me]

    def finish(d, carry):
        share(d).wait()
        out_ref[...] += landed[d]
        return carry

    lax.fori_loop(1, count, finish, 0)


def run_start(flat, x, shards):
    rows, channels = x.shape
    vmem = pl.BlockSpec(memory_space=pltpu.VMEM)
    dma = pltpu.SemaphoreType.DMA
    return pl.pallas_call(
        lambda *refs: start_kernel(shards, *refs),
        in_specs=[vmem] * 2,
        out_specs=[vmem] * 2,
        out_shape=[
            jax.ShapeDtypeStruct((shards,) + flat.shape, F32),
            jax.ShapeDtypeStruct((3 * rows + 2 * EDGE, channels), BF16),
        ],
        scratch_shapes=[dma((shards,)), dma((shards,)), dma((4,)), dma((4,))],
        compiler_params=pltpu.CompilerParams(collective_id=0, has_side_effects=True, **PARAMS),
    )(flat, x)


def run_scatter(packed):
    shards = packed.shape[0]
    vmem = pl.BlockSpec(memory_space=pltpu.VMEM)
    dma = pltpu.SemaphoreType.DMA
    return pl.pallas_call(
        lambda *refs: scatter_kernel(shards, *refs),
        in_specs=[vmem],
        out_specs=vmem,
        out_shape=jax.ShapeDtypeStruct(packed.shape[1:], F32),
        scratch_shapes=[pltpu.VMEM(packed.shape, F32), dma((shards,)), dma((shards,))],
        compiler_params=pltpu.CompilerParams(collective_id=1, has_side_effects=True, **PARAMS),
    )(packed)


def exchange_parts(sections, count, moves, owned, zeros, send, recv, local):
    section, me = lax.axis_index("section"), lax.axis_index("fsdp")

    def device(dsection, steps):
        return {"section": lax.rem(section + dsection + sections, sections), "fsdp": me + steps}

    def copy(i):
        source, first, size, landing, place, dsection, steps = moves[i]
        return pltpu.make_async_remote_copy(
            src_ref=source.at[pl.ds(first, size)],
            dst_ref=landing.at[pl.ds(place, size)],
            send_sem=send.at[i],
            recv_sem=recv.at[i],
            device_id=device(dsection, steps),
        )

    def keep(i):
        source, landing, place = owned[i]
        return pltpu.make_async_copy(
            source, landing.at[pl.ds(place, source.shape[0])], local.at[i]
        )

    def inside(steps):
        return (me + steps >= 0) & (me + steps < count)

    routes = sorted({move[5:] for move in moves})

    def begin():
        barrier = pltpu.get_barrier_semaphore()
        for dsection, steps in routes:

            @pl.when(inside(-steps))
            def _(dsection=dsection, steps=steps):
                pl.semaphore_signal(barrier, inc=1, device_id=device(-dsection, -steps))

        pl.semaphore_wait(barrier, sum(inside(steps).astype(jnp.int32) for _, steps in routes))
        for i, move in enumerate(moves):

            @pl.when(inside(move[6]))
            def _(i=i):
                copy(i).start()

        for i in range(len(owned)):
            keep(i).start()
        zeros[...] = jnp.zeros_like(zeros)
        for i, (_, _, size, landing, place, _, steps) in enumerate(moves):

            @pl.when(jnp.logical_not(inside(-steps)))
            def _(size=size, landing=landing, place=place):
                clear = pltpu.make_async_copy(
                    zeros.at[pl.ds(0, size)],
                    landing.at[pl.ds(place, size)],
                    local.at[len(owned)],
                )
                clear.start()
                clear.wait()

    def finish():
        for i, move in enumerate(moves):

            @pl.when(inside(-move[6]))
            def _(i=i):
                copy(i).wait_recv()

            @pl.when(inside(move[6]))
            def _(i=i):
                copy(i).wait_send()

        for i in range(len(owned)):
            keep(i).wait()

    return begin, finish


def around(begin, finish, body):
    step = pl.program_id(0)
    pl.when(step == 0)(begin)
    body()
    pl.when(step == pl.num_programs(0) - 1)(finish)


def first_forward_kernel(
    sections, count, x_ref, r_ref, gain_ref, short_ref, table_ref, y_ref, e_ref,
    q_ref, k_ref, v_ref, u_ref, w_ref, g_ref, ye_ref, ee_ref, us, ws, zeros, send, recv, local,
):
    rows = y_ref.shape[0]
    moves = (
        (e_ref, 0, rows, ee_ref, rows, 0, -1),
        (e_ref, 0, EDGE, ee_ref, 2 * rows, 0, -2),
        (y_ref, 0, rows, ye_ref, EDGE, 0, 1),
        (y_ref, 0, rows, ye_ref, EDGE + 2 * rows, 0, -1),
        (y_ref, rows - EDGE, EDGE, ye_ref, 0, 0, 2),
        (y_ref, 0, EDGE, ye_ref, EDGE + 3 * rows, 0, -2),
    )
    owned = ((e_ref, ee_ref, 0), (y_ref, ye_ref, EDGE + rows))
    begin, finish = exchange_parts(sections, count, moves, owned, zeros, send, recv, local)
    around(
        begin,
        finish,
        lambda: forward_kernel(
            x_ref, r_ref, gain_ref, short_ref, table_ref,
            q_ref, k_ref, v_ref, u_ref, w_ref, g_ref, us, ws,
        ),
    )


def middle_kernel(sections, count, *refs):
    forward_in, terms_in, d_ref = refs[:5], refs[5:12], refs[12]
    forward_out, terms_out, ee_ref = refs[13:19], refs[19:22], refs[22]
    us, ws, zeros, send, recv, local = refs[23:]
    rows = d_ref.shape[0]
    moves = (
        (d_ref, 0, rows, ee_ref, 0, -1, 0),
        (d_ref, 0, rows, ee_ref, rows, -1, -1),
        (d_ref, 0, EDGE, ee_ref, 2 * rows, -1, -2),
    )
    begin, finish = exchange_parts(sections, count, moves, (), zeros, send, recv, local)

    def body():
        forward_kernel(*forward_in, *forward_out, us, ws)
        terms_kernel(*terms_in, *terms_out)

    around(begin, finish, body)


def forward_specs(total, channels):
    own = TAPS + EDGE
    shapes = [(TAPS + own, F32), (own, F32), (own, F32), (own, F32), (2 * TAPS, BF16), (own, F32)]
    return (
        [tall(total), whole((total, 1)), tall(1), tall(24), GROUP_SPEC],
        [tall(rows) for rows, _ in shapes],
        [jax.ShapeDtypeStruct((rows, channels), kind) for rows, kind in shapes],
        [pltpu.VMEM((total, LANES), F32), pltpu.VMEM((3 * TAPS, LANES), BF16)],
    )


def terms_specs(channels):
    return (
        [
            tall(TAPS), BRANCH_SPEC, tall(TAPS), tall(TAPS + EDGE), tall(2 * TAPS), tall(TAPS),
            whole((TAPS, 1)),
        ],
        [tall(1), tall(24), GROUP_SPEC],
        [
            jax.ShapeDtypeStruct((1, channels), F32),
            jax.ShapeDtypeStruct((24, channels), F32),
            jax.ShapeDtypeStruct((channels // CH_GROUP, 2 * TAPS), F32),
        ],
    )


def exchange_scratch(moves, owned, rows, channels):
    dma = pltpu.SemaphoreType.DMA
    return [pltpu.VMEM((rows, channels), BF16), dma((moves,)), dma((moves,)), dma((owned + 1,))]


def run_first_forward(forward_args, y, e, sections, count):
    rows, channels = y.shape
    ins, outs, shapes, scratch = forward_specs(forward_args[0].shape[0], channels)
    remote = pl.BlockSpec(memory_space=pl.ANY)
    return pl.pallas_call(
        lambda *refs: first_forward_kernel(sections, count, *refs),
        grid=(channels // LANES,),
        in_specs=ins + [remote] * 2,
        out_specs=outs + [remote] * 2,
        out_shape=shapes
        + [
            jax.ShapeDtypeStruct((3 * rows + 2 * EDGE, channels), BF16),
            jax.ShapeDtypeStruct((2 * rows + EDGE, channels), BF16),
        ],
        scratch_shapes=scratch + exchange_scratch(6, 2, rows, channels),
        compiler_params=pltpu.CompilerParams(collective_id=2, has_side_effects=True, **PARAMS),
    )(*forward_args, y, e)


def run_middle(forward_args, terms_args, d, sections, count):
    rows, channels = d.shape
    ins, outs, shapes, scratch = forward_specs(forward_args[0].shape[0], channels)
    more_ins, more_outs, more_shapes = terms_specs(channels)
    remote = pl.BlockSpec(memory_space=pl.ANY)
    return pl.pallas_call(
        lambda *refs: middle_kernel(sections, count, *refs),
        grid=(channels // LANES,),
        in_specs=ins + more_ins + [remote],
        out_specs=outs + more_outs + [remote],
        out_shape=shapes
        + more_shapes
        + [jax.ShapeDtypeStruct((2 * rows + EDGE, channels), BF16)],
        scratch_shapes=scratch + exchange_scratch(3, 0, rows, channels),
        compiler_params=pltpu.CompilerParams(collective_id=3, has_side_effects=True, **PARAMS),
    )(*forward_args, *terms_args, d)


def on_device(
    inputs, top_grad, gains, short_filters, medium_filters, lower_gain, lower_short, lower_medium
):
    shards = lax.axis_size("fsdp")
    last_section = lax.axis_index("section") == lax.axis_size("section") - 1
    chunk = gains.shape[1]
    channels = chunk * shards
    flat = jnp.stack(
        [
            jnp.concatenate([gains.reshape(-1), short_filters.reshape(-1), medium_filters[0].T.reshape(-1)]),
            jnp.concatenate([lower_gain, lower_short.reshape(-1), lower_medium.T.reshape(-1)]),
        ]
    )
    x1, x2, e1 = inputs[0, 0], inputs[1, 0], top_grad[0]
    extent = flat.shape[1]
    room = -(-extent // 1024) * 1024
    flat = jnp.pad(flat, ((0, 0), (0, room - extent))).reshape(-1, LANES)
    every, x1_ext = run_start(flat, x1, shards)
    by_rows = chunk == LANES
    every = every.reshape(shards, 2, room // LANES, LANES)

    def layer_params(part):
        if by_rows:
            gain, short, medium = part[:, :1], part[:, 1:22], part[:, 22:30]
        else:
            part = part.reshape(shards, room)
            gain, short = part[:, :chunk], part[:, chunk : 22 * chunk]
            medium = part[:, 22 * chunk : extent]
        gain = gain.reshape(1, channels)
        short = jnp.transpose(short.reshape(shards, 3 * SHORT, chunk), (1, 0, 2))
        short = short.reshape(3 * SHORT, channels)
        medium = medium.reshape(TAPS, -1).T
        medium = medium.astype(BF16).astype(F32)
        short = jnp.pad(short, ((0, 3), (0, 0)))
        causal = jnp.pad(medium[:, ::-1], ((0, 0), (1, TAPS - 1)))
        anti = jnp.pad(medium, ((0, 0), (0, TAPS)))
        return gain, short, causal, anti

    upper = every[:, 0]
    params = (layer_params(upper), layer_params(jnp.where(last_section, every[:, 1], upper)))

    def row_scale(x_ext):
        wide = x_ext.astype(F32)
        return lax.rsqrt(jnp.mean(wide * wide, axis=-1, keepdims=True) + NORM_EPS)

    own_rows = slice(TAPS + EDGE, 2 * TAPS + EDGE)
    (gain1, short1, causal1, anti1), (gain2, short2, causal2, anti2) = params
    sections = lax.axis_size("section")
    r1_ext = row_scale(x1_ext)
    r1 = r1_ext[own_rows]
    *ahead1, x2_ext, e1_ext = run_first_forward(
        (x1_ext, r1_ext, gain1, short1, causal1), x2, e1, sections, shards
    )
    r2_ext = row_scale(x2_ext)
    r2 = r2_ext[own_rows]
    dx1, *back1 = run_backward(
        e1_ext, ahead1[0], ahead1[1], ahead1[2], ahead1[5], x1, r1, gain1, short1, anti1
    )
    middle = run_middle(
        (x2_ext, r2_ext, gain2, short2, causal2),
        (*back1, ahead1[3], ahead1[4], x1, r1),
        dx1,
        sections,
        shards,
    )
    ahead2, terms1, e2_ext = middle[:6], middle[6:9], middle[9]
    dx2, *back2 = run_backward(
        e2_ext, ahead2[0], ahead2[1], ahead2[2], ahead2[5], x2, r2, gain2, short2, anti2
    )
    terms2 = run_terms(*back2, ahead2[3], ahead2[4], x2, r2)
    keep = jnp.where(last_section, 0.0, 1.0)
    tg, ts, tm = [a + keep * b for a, b in zip(terms1, terms2)]
    ts = jnp.transpose(ts[: 3 * SHORT].reshape(3 * SHORT, shards, chunk), (1, 0, 2))
    tm = tm[:, 1 : TAPS + 1][:, ::-1]
    groups = tm.shape[0]
    tm = tm.T
    packed = jnp.concatenate(
        [tg.reshape(shards, chunk), ts.reshape(shards, -1), tm.reshape(shards, -1)], axis=1
    )
    factor = (x1.shape[0] * shards) ** (-0.5)
    width = packed.shape[1]
    room = -(-width // 1024) * 1024
    packed = jnp.pad(packed, ((0, 0), (0, room - width))).reshape(shards, -1, LANES)
    summed = run_scatter(packed).reshape(-1) * factor
    return (
        dx2[None],
        summed[:chunk][None],
        summed[chunk : 22 * chunk].reshape(1, 3, SHORT, chunk),
        summed[22 * chunk : 30 * chunk].reshape(TAPS // shards, groups).T[None],
    )


def solution(mesh):
    in_specs = (
        P(None, "section", "fsdp", None),
        P("section", "fsdp", None),
        P("section", "fsdp"),
        P("section", None, None, "fsdp"),
        P("section", None, "fsdp"),
        P("fsdp"),
        P(None, None, "fsdp"),
        P(None, "fsdp"),
    )
    out_specs = (
        P("section", "fsdp", None),
        P("section", "fsdp"),
        P("section", None, None, "fsdp"),
        P("section", None, "fsdp"),
    )
    return jax.shard_map(
        on_device, mesh=mesh, in_specs=in_specs, out_specs=out_specs, check_vma=False
    )
```
